256 devices in a mesh: dp: 16 (over z, core), tensor: 16 (over y, x).
Axes of the slice: x: 4, y: 4, z: 8, core: 2. Of those that a mesh axis runs over, the one named last changes fastest.
Arguments:
- activations: bfloat16 [36864, 8192], P('dp', 'tensor'), may hold values from -6 to 6
- out_grads: bfloat16 [36864, 28672], P('dp', 'tensor'), may hold values from -0.0546875 to 0.0546875
- basis: bfloat16 [8192, 256], P('tensor'), may hold values from -0.375 to 0.375
- first_moment: float32 [256, 28672], P('dp', 'tensor'), may hold values from -6 to 6
- second_moment: float32 [256, 28672], P('dp', 'tensor'), may hold values from 0.05 to 0.8
- reward_codes: int32 [36864], P('dp'), may hold values from 0 to 15
- token_ids: int32 [36864], P('dp'), may hold values from 0 to 128004, as said below
Outputs:
- new_first: float32 [256, 28672], P('dp', 'tensor')
- new_second: float32 [256, 28672], P('dp', 'tensor')
- weight_update: bfloat16 [8192, 28672], P('dp', 'tensor')
The draws below stay inside these ranges and needn't reach their ends.
Inputs may be any that keep to these rules, and one draw needn't show every extreme that they name: `token_ids`: the id 128004 is the padding token; the first of each 2304 consecutive tokens is never padding.
All inputs are finite; a program needn't handle non-finite values.
Results may differ from the reference program's by a relative error of at most 0.019.
Values may be sent and summed in bfloat16 or wider, within the bound.
A program may use at most 64 MiB of HBM per device.

```python
import math
import jax
import jax.numpy as jnp
from jax import lax

D = 8192
FF = 28672
R = 256
TOK_DEV = 2304
LEVELS = 16
ADAM_STEP = 100
TOKENS = 36864
N_TENSOR = 16


pad_token = 128004


def draw_reward_codes(key, part):
    code_key = jax.random.fold_in(key, 7)
    positions = jnp.arange(TOKENS, dtype=jnp.int32)
    block_count = TOKENS // TOK_DEV
    block_index = positions // TOK_DEV
    baseline = jax.random.randint(code_key, (TOKENS,), 0, LEVELS // 2, dtype=jnp.int32)
    ramp = block_index * (LEVELS // 2) // max(block_count - 1, 1)
    return (baseline + ramp).astype(jnp.int32)


def draw_token_ids(key, part):
    id_key = jax.random.fold_in(key, 11)
    mask_key = jax.random.fold_in(key, 12)
    rate_key = jax.random.fold_in(key, 13)
    positions = jnp.arange(TOKENS, dtype=jnp.int32)
    block_count = TOKENS // TOK_DEV
    block_index = positions // TOK_DEV
    block_rates = jax.random.randint(rate_key, (block_count,), 0, 9, dtype=jnp.int32)
    token_rates = jnp.take(block_rates, block_index)
    plain_ids = jax.random.randint(id_key, (TOKENS,), 0, pad_token, dtype=jnp.int32)
    chosen = jax.random.randint(mask_key, (TOKENS,), 0, 16, dtype=jnp.int32) < token_rates
    padded = chosen & (positions % TOK_DEV != 0)
    return jnp.where(padded, pad_token, plain_ids).astype(jnp.int32)


def block_scale(stream_key, extent, shards, smallest, largest):
    def one(dim, blocks):
        heights = jax.random.uniform(jax.random.fold_in(jax.random.fold_in(stream_key, 6), dim), (blocks,), jnp.float32, smallest / len(shards), largest / len(shards))
        return jnp.repeat(jnp.exp(heights), extent[dim] // blocks).reshape((-1,) + (1,) * (len(extent) - dim - 1))

    factor_of = one(*shards[0])
    for cut in shards[1:]:
        factor_of = factor_of * one(*cut)
    return factor_of


def noise(rng, dims, deviation, bound, shards=(), kind=jnp.bfloat16):
    array = deviation * jax.random.normal(rng, dims, jnp.float32)
    if shards:
        array = array * block_scale(rng, dims, shards, -0.22, 0.18)
    return jnp.clip(array, -bound, bound).astype(kind)


def setup_inputs(seed: int = 0) -> dict:
    seeds = jax.random.split(jax.random.key(seed), 8)
    return {
        "activations": noise(seeds[0], (TOKENS, D), 1.0, 6.0, ((0, 16), (1, 16))),
        "out_grads": noise(seeds[1], (TOKENS, FF), (4 * (D * TOKENS // R) ** -0.5), 0.0546875, ((0, 16), (1, 16))),
        "basis": noise(seeds[2], (D, R), R ** -0.5, 0.375, ((0, 16),)),
        "first_moment": noise(seeds[3], (R, FF), 1.0, 6.0, ((0, 16), (1, 16)), jnp.float32),
        "second_moment": jnp.clip(jnp.exp(math.log(0.8) - 2.7725887 * jax.random.uniform(seeds[4], (R, FF), jnp.float32) ** block_scale(seeds[4], (R, FF), ((0, 16), (1, 16)), -0.2, 0.2)), 0.05, 0.8),
        "reward_codes": draw_reward_codes(jax.random.fold_in(seeds[7], 71), 0),
        "token_ids": draw_token_ids(jax.random.fold_in(seeds[7], 71), 0),
    }


pad_token = 128004
reward_temp = 0.2
beta_one = 0.9
beta_two = 0.999
adam_eps = 1e-08

def reference(activations, out_grads, basis, first_moment, second_moment, reward_codes, token_ids):
    block_width = D // N_TENSOR
    projected = jnp.zeros((TOKENS, R), jnp.float32)
    for position in range(N_TENSOR):
        lower = position * block_width
        part_sum = jnp.dot(activations[:, lower:lower + block_width], basis[lower:lower + block_width, :], preferred_element_type=jnp.float32)
        rounded = lax.optimization_barrier(part_sum.astype(jnp.bfloat16))
        projected = projected + rounded.astype(jnp.float32)
    unmasked = (token_ids != pad_token).astype(jnp.float32)
    weights = unmasked * jnp.exp(reward_temp * reward_codes.astype(jnp.float32))
    normalizer = jnp.sum(weights)
    weighted = (weights[:, None] * projected).astype(jnp.bfloat16)
    raw_gradient = lax.dot_general(weighted, out_grads, (((0,), (0,)), ((), ())), preferred_element_type=jnp.float32)
    gradient = raw_gradient * (TOKENS / normalizer)
    new_first = beta_one * first_moment + (1.0 - beta_one) * gradient
    new_second = beta_two * second_moment + (1.0 - beta_two) * gradient * gradient
    bias_one = 1.0 - beta_one ** ADAM_STEP
    bias_two = 1.0 - beta_two ** ADAM_STEP
    update = (new_first / bias_one / (jnp.sqrt(new_second / bias_two) + adam_eps)).astype(jnp.bfloat16)
    weight_update = jnp.dot(basis, update, preferred_element_type=jnp.float32).astype(jnp.bfloat16)
    return (new_first, new_second, weight_update)
```

```python
import jax
import jax.numpy as jnp
from jax import lax
from jax.experimental import pallas as pl
from jax.experimental.pallas import tpu as pltpu
from jax.sharding import PartitionSpec as P

ADAM_STEP = 100
PAD = 128004
TEMP = 0.2
B1 = 0.9
B2 = 0.999
EPS = 1e-8
MESH = pl.DeviceIdType.MESH
F32 = jnp.float32
BF16 = jnp.bfloat16

NX = NY = 4
NZ = 8
TOK = 2304
HALF = TOK // 2
D = 512
R = 256
FF = 1792
ROWS = 16
BLK = R // NX
HB = BLK // 2
CUT = (0, 1024, FF)
WID = (1024, 768)
TOKENS = TOK * 16
SLOT = {4: 0, 3: 1, 5: 2, 2: 3, 6: 4, 1: 5, 7: 6, 0: 7}
PIECES = ((0, 3), (3, 2), (5, 3))


def rows(ref, start, size):
    return ref.at[pl.ds(pl.multiple_of(start, 16), size)]


def load(ref, start, size):
    return ref[pl.ds(pl.multiple_of(start, 16), size), :].astype(F32)


def kernel(
    act, og, basis, m1, m2, codes, ids, nf_o, ns_o, wu_o,
    act_v, og_v, basis_v, basis_t, m1_v, m2_v, codes_v, ids_v, wrow,
    px, py, wx, wy, r1, t1, s1, r2, raw,
    nsend, nrecv, cs0, cs1, cr0, cr1,
    tx0, tx1, rx0, rx1, u0, u1, own_v, nf_v, ns_v, wu_v,
    lsem, osem, xs, xr, nss, nrs, ces, cer, zs, zr, gs, gr, fs, fr, bs, br, bl,
):
    dp = lax.axis_index("dp")
    tn = lax.axis_index("tensor")
    z, c = dp // 2, dp % 2
    y, x = tn // NX, tn % NX

    def at(dx=0, dy=0, dz=0, dc=0):
        return (
            ((z + dz) % NZ) * 2 + (c + dc) % 2,
            ((y + dy) % NY) * NX + (x + dx) % NX,
        )

    partners = [at(dx=j) for j in (1, 2, 3)] + [at(dy=j) for j in (1, 2, 3)]
    partners += [at(dz=1), at(dz=NZ - 1), at(dc=1)]
    barrier = pltpu.get_barrier_semaphore()
    for other in partners:
        pl.semaphore_signal(barrier, inc=1, device_id=other, device_id_type=MESH)

    pending = []

    def send(src, dst, ssem, rsem, to):
        copy = pltpu.make_async_remote_copy(
            src_ref=src, dst_ref=dst, send_sem=ssem, recv_sem=rsem,
            device_id=to, device_id_type=MESH,
        )
        copy.start()
        pending.append(copy)
        return copy

    def fetch(src, dst, n):
        copy = pltpu.make_async_copy(src, dst, lsem.at[n])
        copy.start()
        return copy

    f_basis = fetch(basis, basis_v, 0)
    step = TOK // 6
    f_act = [
        fetch(act.at[pl.ds(i * step, step)], act_v.at[pl.ds(i * step, step)], 1 + i)
        for i in range(6)
    ]
    f_codes = fetch(codes, codes_v, 7)
    f_ids = fetch(ids, ids_v, 8)
    f_m1 = fetch(m1, m1_v, 9)
    f_m2 = fetch(m2, m2_v, 10)
    f_og = [
        fetch(og.at[pl.ds(i * HALF, HALF)], og_v.at[pl.ds(i * HALF, HALF)], 11 + i)
        for i in range(2)
    ]

    f_basis.wait()
    basis_t[...] = basis_v[...].T
    for i in range(6):
        f_act[i].wait()
        part = lax.dot_general(
            basis_t[...], act_v[i * step : (i + 1) * step, :],
            (((1,), (1,)), ((), ())), preferred_element_type=F32,
        ).astype(BF16)
        into = px if i < 3 else py
        into[:, (i % 3) * step : (i % 3 + 1) * step] = part

    pl.semaphore_wait(barrier, len(partners))

    class Unit:
        pass

    units = []
    for n, (p, w, pf, ps) in enumerate(((px, wx, x, y), (py, wy, y, x))):
        u = Unit()
        u.n, u.p, u.w, u.pf, u.ps = n, p, w, pf, ps
        u.first = (lambda j: at(dx=j % 4)) if n == 0 else (lambda j: at(dy=j % 4))
        u.second = (lambda j: at(dy=j % 4)) if n == 0 else (lambda j: at(dx=j % 4))
        u.r1, u.t1, u.s1, u.r2 = r1.at[n], t1.at[n], s1.at[n], r2.at[n]
        u.sem = lambda i, n=n: (xs.at[n, i], xr.at[n, i])
        units.append(u)

    def stage1(u):
        q2, qr, ql = (u.pf + 2) % 4, (u.pf + 1) % 4, (u.pf + 3) % 4
        u.a = [None] * 6
        u.a[0] = send(rows(u.p, q2 * BLK, HB), u.r1.at[0], *u.sem(0), u.first(1))
        u.a[3] = send(rows(u.p, q2 * BLK + HB, HB), u.r1.at[3], *u.sem(3), u.first(3))
        u.a[1] = send(rows(u.p, qr * BLK + HB, HB), u.r1.at[1], *u.sem(1), u.first(1))
        u.a[4] = send(rows(u.p, ql * BLK, HB), u.r1.at[4], *u.sem(4), u.first(3))

    def stage2(u):
        qr, ql = (u.pf + 1) % 4, (u.pf + 3) % 4
        u.a[0].wait_recv()
        u.t1[0] = (load(u.p, qr * BLK, HB) + u.r1[0].astype(F32)).astype(BF16)
        u.a[2] = send(u.t1.at[0], u.r1.at[2], *u.sem(2), u.first(1))
        u.a[3].wait_recv()
        u.t1[1] = (load(u.p, ql * BLK + HB, HB) + u.r1[3].astype(F32)).astype(BF16)
        u.a[5] = send(u.t1.at[1], u.r1.at[5], *u.sem(5), u.first(3))

    def stage3(u):
        for i in (1, 4, 2, 5):
            u.a[i].wait_recv()
        low = load(u.p, u.pf * BLK, HB) + u.r1[2].astype(F32) + u.r1[4].astype(F32)
        u.s1[0:HB, :] = low.astype(BF16)
        high = load(u.p, u.pf * BLK + HB, HB) + u.r1[1].astype(F32) + u.r1[5].astype(F32)
        u.s1[HB:BLK, :] = high.astype(BF16)
        u.b = [
            send(rows(u.s1, ((u.ps + j) % 4) * ROWS, ROWS), u.r2.at[j - 1], *u.sem(5 + j), u.second(j))
            for j in (1, 2, 3)
        ]

    def stage4(u):
        for copy in u.b:
            copy.wait_recv()
        total = load(u.s1, u.ps * ROWS, ROWS)
        for j in range(3):
            total = total + u.r2[j].astype(F32)
        total = total * wrow[:, u.n * HALF : (u.n + 1) * HALF]
        mine = u.pf * BLK + u.ps * ROWS
        u.w[pl.ds(pl.multiple_of(mine, 16), ROWS), :] = total.astype(BF16)
        u.c = [
            send(rows(u.w, mine, ROWS), rows(u.w, mine, ROWS), *u.sem(8 + j), u.second(j))
            for j in (1, 2, 3)
        ]

    def stage5(u):
        for copy in u.c:
            copy.wait_recv()
        low, high = rows(u.w, u.pf * BLK, HB), rows(u.w, u.pf * BLK + HB, HB)
        u.d = [None] * 6
        u.d[0] = send(low, low, *u.sem(12), u.first(1))
        u.d[3] = send(high, high, *u.sem(15), u.first(3))
        u.d[1] = send(high, high, *u.sem(13), u.first(1))
        u.d[4] = send(low, low, *u.sem(16), u.first(3))

    def stage6(u):
        u.d[0].wait_recv()
        low = rows(u.w, ((u.pf + 3) % 4) * BLK, HB)
        u.d[2] = send(low, low, *u.sem(14), u.first(1))
        u.d[3].wait_recv()
        high = rows(u.w, ((u.pf + 1) % 4) * BLK + HB, HB)
        u.d[5] = send(high, high, *u.sem(17), u.first(3))

    def stage7(u):
        for i in (1, 4, 2, 5):
            u.d[i].wait_recv()

    for u in units:
        stage1(u)

    f_codes.wait()
    f_ids.wait()
    weights = jnp.where(ids_v[...] == PAD, 0.0, jnp.exp(TEMP * codes_v[...].astype(F32)))
    for i in range(TOK // 128):
        wrow[:, i * 128 : (i + 1) * 128] = jnp.broadcast_to(weights[i : i + 1, :], (ROWS, 128))
    local = jnp.sum(jnp.sum(weights, axis=0, keepdims=True), axis=1, keepdims=True)
    nsend[0] = jnp.broadcast_to(local, (8, 128))
    ncore = send(nsend.at[0], nrecv.at[7], nss.at[7], nrs.at[7], at(dc=1))

    for u in units:
        stage2(u)
    ncore.wait_recv()
    nsend[1] = nsend[0] + nrecv[7]
    nr = send(nsend.at[1], nrecv.at[0], nss.at[0], nrs.at[0], at(dz=1))
    nl = send(nsend.at[1], nrecv.at[4], nss.at[4], nrs.at[4], at(dz=NZ - 1))
    for u in units:
        stage3(u)

    def norm_hop(i, nr, nl):
        nr.wait_recv()
        nr = send(nrecv.at[i - 1], nrecv.at[i], nss.at[i], nrs.at[i], at(dz=1))
        if i < 3:
            nl.wait_recv()
            nl = send(nrecv.at[3 + i], nrecv.at[4 + i], nss.at[4 + i], nrs.at[4 + i], at(dz=NZ - 1))
        return nr, nl

    nr, nl = norm_hop(1, nr, nl)
    for u in units:
        stage4(u)
    nr, nl = norm_hop(2, nr, nl)
    for u in units:
        stage5(u)
    nr, nl = norm_hop(3, nr, nl)
    for u in units:
        stage6(u)
    nr.wait_recv()
    nl.wait_recv()
    scale = nsend[1]
    for i in range(7):
        scale = scale + nrecv[i]
    scale = TOKENS / scale[0:1, 0:1]
    for copy in f_og:
        copy.wait()
    for u in units:
        stage7(u)

    x0, y0 = dp % NX, dp // NX
    in_row, in_col = y == y0, x == x0
    is_src = jnp.logical_and(in_row, in_col)
    parts = (pl.ds(0, D // 2), pl.ds(D // 2, D // 2))
    hop = ((lambda j: at(dx=j), lambda j: at(dy=j)), (lambda j: at(dy=j), lambda j: at(dx=j)))
    member = (in_row, in_col)

    def spread(h, level, src):
        copies = []
        for j in (1, 2, 3):
            i = h * 6 + level * 3 + j - 1
            copies.append(
                pltpu.make_async_remote_copy(
                    src_ref=src.at[parts[h]], dst_ref=own_v.at[parts[h]],
                    send_sem=bs.at[i], recv_sem=br.at[h],
                    device_id=hop[h][level](j), device_id_type=MESH,
                )
            )
        return copies

    def basis_first():
        @pl.when(is_src)
        def _():
            pltpu.make_async_copy(basis_v, own_v, bl).start()
            for h in (0, 1):
                for copy in spread(h, 0, basis_v):
                    copy.start()
            for h in (0, 1):
                for copy in spread(h, 1, basis_v):
                    copy.start()

    def basis_second():
        for h in (0, 1):
            @pl.when(jnp.logical_and(member[h], jnp.logical_not(is_src)))
            def _(h=h):
                copies = spread(h, 1, own_v)
                copies[0].wait_recv()
                for copy in copies:
                    copy.start()

    def basis_last():
        @pl.when(is_src)
        def _():
            pltpu.make_async_copy(basis_v, own_v, bl).wait()
            for h in (0, 1):
                for copy in spread(h, 0, basis_v):
                    copy.wait_send()

        for h in (0, 1):
            copies = spread(h, 1, own_v)

            @pl.when(jnp.logical_not(member[h]))
            def _(copies=copies):
                copies[0].wait_recv()

            @pl.when(member[h])
            def _(copies=copies):
                for copy in copies:
                    copy.wait_send()

    cs, cr, tx, rx, up = (cs0, cs1), (cr0, cr1), (tx0, tx1), (rx0, rx1), (u0, u1)
    exch = [[], []]

    def block_of(k, core):
        return (((z + k) % NZ) * 2 + core) * ROWS

    def raw_columns(h):
        for lo in range(CUT[h], CUT[h + 1], 256):
            raw[:, lo : lo + 256] = jnp.dot(
                wx[...], og_v[0:HALF, lo : lo + 256], preferred_element_type=F32
            ) + jnp.dot(wy[...], og_v[HALF:TOK, lo : lo + 256], preferred_element_type=F32)
        for n, (at_slot, count) in enumerate(PIECES):
            for k, slot in SLOT.items():
                if at_slot <= slot < at_slot + count:
                    cs[h][slot] = raw[
                        pl.ds(pl.multiple_of(block_of(k, 1 - c), 16), ROWS), CUT[h] : CUT[h + 1]
                    ].astype(BF16)
            span = pl.ds(at_slot, count)
            exch[h].append(
                send(cs[h].at[span], cr[h].at[span], ces.at[h, n], cer.at[h, n], at(dc=1))
            )

    def chip_sum(k, h):
        mine = raw[pl.ds(pl.multiple_of(block_of(k, c), 16), ROWS), CUT[h] : CUT[h + 1]]
        return mine + cr[h][SLOT[k]].astype(F32)

    arrived = {}

    def ring_send(h, way, s):
        length = 4 if way == h else 3
        if s > length:
            return
        k = (length + 1 - s) if way == 0 else (NZ - (length + 1 - s))
        total = chip_sum(k, h)
        if s > 1:
            arrived[h, way].wait_recv()
            total = total + rx[h][way * 4 + s - 2].astype(F32)
        i = way * 4 + s - 1
        tx[h][i] = total.astype(BF16)
        arrived[h, way] = send(
            tx[h].at[i], rx[h].at[i], zs.at[h, i], zr.at[h, i], at(dz=1 if way == 0 else NZ - 1)
        )

    basis_first()
    for h in (0, 1):
        raw_columns(h)
        exch[h][0].wait_recv()
        for way in (h, 1 - h):
            ring_send(h, way, 1)
    basis_second()
    for h in (0, 1):
        exch[h][1].wait_recv()
        exch[h][2].wait_recv()
    for s in (2, 3, 4):
        for h in (0, 1):
            for way in (h, 1 - h):
                ring_send(h, way, s)

    bias1 = 1.0 - B1**ADAM_STEP
    bias2 = 1.0 - B2**ADAM_STEP
    f_m1.wait()
    f_m2.wait()

    outs = []

    def store(src, dst, n):
        copy = pltpu.make_async_copy(src, dst, osem.at[n])
        copy.start()
        outs.append(copy)

    forwards = {}
    gathered = {}

    def gather_send(h, way, s):
        length = 4 if way == h else 3
        if s > length:
            return
        origin = (z + (NZ - (s - 1) if way == 0 else s - 1)) % NZ
        block = up[h].at[origin * 2 + c]
        i = way * 4 + s - 1
        gathered[h, way, s] = send(
            block, block, gs.at[h, i], gr.at[h, i], at(dz=1 if way == 0 else NZ - 1)
        )

    def forward(h, off):
        block = up[h].at[((z + off) % NZ) * 2 + c]
        forwards[h, off] = send(block, block, fs.at[h, off], fr.at[h, off], at(dc=1))

    for h in (0, 1):
        for way in (0, 1):
            arrived[h, way].wait_recv()
        last = (3 if h == 0 else 2, 4 + (3 if h == 1 else 2))
        grad = chip_sum(0, h) + rx[h][last[0]].astype(F32) + rx[h][last[1]].astype(F32)
        grad = grad * scale
        cols = slice(CUT[h], CUT[h + 1])
        first = B1 * m1_v[:, cols] + (1.0 - B1) * grad
        second = B2 * m2_v[:, cols] + (1.0 - B2) * grad * grad
        up[h][dp] = ((first / bias1) / (jnp.sqrt(second / bias2) + EPS)).astype(BF16)
        for way in (h, 1 - h):
            gather_send(h, way, 1)
        forward(h, 0)
        nf_v[:, cols] = first
        ns_v[:, cols] = second
    store(nf_v, nf_o, 0)
    store(ns_v, ns_o, 1)
    for s in (1, 2, 3, 4):
        for h in (0, 1):
            for way in (h, 1 - h):
                if (h, way, s) in gathered:
                    gathered[h, way, s].wait_recv()
                    gather_send(h, way, s + 1)
                    forward(h, (NZ - s) % NZ if way == 0 else s)
    basis_last()
    for h in (0, 1):
        for off in range(NZ):
            forwards[h, off].wait_recv()
        for lo in range(0, WID[h], 256):
            wu_v[:, CUT[h] + lo : CUT[h] + lo + 256] = jnp.dot(
                own_v[...], up[h][:, :, lo : lo + 256].reshape(R, 256), preferred_element_type=F32
            ).astype(BF16)
        cols = pl.ds(CUT[h], WID[h])
        store(wu_v.at[:, cols], wu_o.at[:, cols], 2 + h)
    for copy in pending:
        copy.wait_send()
    for copy in outs:
        copy.wait()


def local(activations, out_grads, basis, first_moment, second_moment, reward_codes, token_ids):
    any_ = pl.BlockSpec(memory_space=pl.ANY)
    vm = pltpu.VMEM
    dma = pltpu.SemaphoreType.DMA
    return pl.pallas_call(
        kernel,
        out_shape=(
            jax.ShapeDtypeStruct((ROWS, FF), F32),
            jax.ShapeDtypeStruct((ROWS, FF), F32),
            jax.ShapeDtypeStruct((D, FF), BF16),
        ),
        in_specs=[any_] * 7,
        out_specs=(any_, any_, any_),
        scratch_shapes=[
            vm((TOK, D), BF16), vm((TOK, FF), BF16), vm((D, R), BF16), vm((R, D), BF16),
            vm((ROWS, FF), F32), vm((ROWS, FF), F32),
            vm((TOK // 128, 128), jnp.int32), vm((TOK // 128, 128), jnp.int32),
            vm((ROWS, TOK), F32),
            vm((R, HALF), BF16), vm((R, HALF), BF16), vm((R, HALF), BF16), vm((R, HALF), BF16),
            vm((2, 6, HB, HALF), BF16), vm((2, 2, HB, HALF), BF16), vm((2, BLK, HALF), BF16),
            vm((2, 3, ROWS, HALF), BF16), vm((R, FF), F32),
            vm((2, 8, 128), F32), vm((8, 8, 128), F32),
            vm((8, ROWS, WID[0]), BF16), vm((8, ROWS, WID[1]), BF16),
            vm((8, ROWS, WID[0]), BF16), vm((8, ROWS, WID[1]), BF16),
            vm((8, ROWS, WID[0]), BF16), vm((8, ROWS, WID[1]), BF16),
            vm((8, ROWS, WID[0]), BF16), vm((8, ROWS, WID[1]), BF16),
            vm((16, ROWS, WID[0]), BF16), vm((16, ROWS, WID[1]), BF16),
            vm((D, R), BF16), vm((ROWS, FF), F32), vm((ROWS, FF), F32), vm((D, FF), BF16),
            dma((13,)), dma((4,)), dma((2, 18)), dma((2, 18)), dma((8,)), dma((8,)),
            dma((2, 3)), dma((2, 3)), dma((2, 8)), dma((2, 8)), dma((2, 8)), dma((2, 8)),
            dma((2, 8)), dma((2, 8)), dma((12,)), dma((2,)), dma,
        ],
        compiler_params=pltpu.CompilerParams(
            collective_id=0, has_side_effects=True, vmem_limit_bytes=48 * 1024 * 1024
        ),
        name="galore_step",
    )(
        activations, out_grads, basis, first_moment, second_moment,
        reward_codes.reshape(TOK // 128, 128), token_ids.reshape(TOK // 128, 128),
    )


def solution(mesh):
    return jax.shard_map(
        local,
        mesh=mesh,
        in_specs=(
            P("dp", "tensor"),
            P("dp", "tensor"),
            P("tensor", None),
            P("dp", "tensor"),
            P("dp", "tensor"),
            P("dp"),
            P("dp"),
        ),
        out_specs=(P("dp", "tensor"), P("dp", "tensor"), P("dp", "tensor")),
        check_vma=False,
    )
```

```python
import jax
import jax.numpy as jnp
from jax import lax
from jax.experimental import pallas as pl
from jax.experimental.pallas import tpu as pltpu
from jax.sharding import PartitionSpec as P

ADAM_STEP = 100
PAD = 128004
TEMP = 0.2
B1 = 0.9
B2 = 0.999
EPS = 1e-8
MESH = pl.DeviceIdType.MESH
F32 = jnp.float32
BF16 = jnp.bfloat16

NX = NY = 4
NZ = 8
TOK = 2304
HALF = TOK // 2
D = 512
R = 256
FF = 1792
ROWS = 16
BLK = R // NX
HB = BLK // 2
CUT = (0, 1024, FF)
WID = (1024, 768)
TOKENS = TOK * 16
SLOT = {4: 0, 3: 1, 5: 2, 2: 3, 6: 4, 1: 5, 7: 6, 0: 7}
PIECES = ((0, 3), (3, 2), (5, 3))


def rows(ref, start, size):
    return ref.at[pl.ds(pl.multiple_of(start, 16), size)]


def load(ref, start, size):
    return ref[pl.ds(pl.multiple_of(start, 16), size), :].astype(F32)


def kernel(
    act, og, basis, m1, m2, codes, ids, nf_v, ns_v, own_v, u0, u1,
    act_v, og_v, basis_v, basis_t, m1_v, m2_v, codes_v, ids_v, wrow,
    px, py, wx, wy, r1, t1, s1, r2, raw,
    nsend, nrecv, cs0, cs1, cr0, cr1,
    tx0, tx1, rx0, rx1,
    lsem, xs, xr, nss, nrs, ces, cer, zs, zr, gs, gr, fs, fr, bs, br, bl,
):
    dp = lax.axis_index("dp")
    tn = lax.axis_index("tensor")
    z, c = dp // 2, dp % 2
    y, x = tn // NX, tn % NX

    def at(dx=0, dy=0, dz=0, dc=0):
        return (
            ((z + dz) % NZ) * 2 + (c + dc) % 2,
            ((y + dy) % NY) * NX + (x + dx) % NX,
        )

    partners = [at(dx=j) for j in (1, 2, 3)] + [at(dy=j) for j in (1, 2, 3)]
    partners += [at(dz=j) for j in range(1, NZ)] + [at(dc=1)]
    barrier = pltpu.get_barrier_semaphore()
    for other in partners:
        pl.semaphore_signal(barrier, inc=1, device_id=other, device_id_type=MESH)

    pending = []

    def send(src, dst, ssem, rsem, to):
        copy = pltpu.make_async_remote_copy(
            src_ref=src, dst_ref=dst, send_sem=ssem, recv_sem=rsem,
            device_id=to, device_id_type=MESH,
        )
        copy.start()
        pending.append(copy)
        return copy

    def fetch(src, dst, n):
        copy = pltpu.make_async_copy(src, dst, lsem.at[n])
        copy.start()
        return copy

    f_basis = fetch(basis, basis_v, 0)
    step = TOK // 6
    f_act = [
        fetch(act.at[pl.ds(i * step, step)], act_v.at[pl.ds(i * step, step)], 1 + i)
        for i in range(6)
    ]
    f_codes = fetch(codes, codes_v, 7)
    f_ids = fetch(ids, ids_v, 8)
    f_m1 = fetch(m1, m1_v, 9)
    f_m2 = fetch(m2, m2_v, 10)
    f_og = [
        fetch(og.at[pl.ds(i * HALF, HALF)], og_v.at[pl.ds(i * HALF, HALF)], 11 + i)
        for i in range(2)
    ]

    f_basis.wait()
    basis_t[...] = basis_v[...].T
    for i in range(6):
        f_act[i].wait()
        part = lax.dot_general(
            basis_t[...], act_v[i * step : (i + 1) * step, :],
            (((1,), (1,)), ((), ())), preferred_element_type=F32,
        ).astype(BF16)
        into = px if i < 3 else py
        into[:, (i % 3) * step : (i % 3 + 1) * step] = part

    pl.semaphore_wait(barrier, len(partners))

    class Unit:
        pass

    units = []
    for n, (p, w, pf, ps) in enumerate(((px, wx, x, y), (py, wy, y, x))):
        u = Unit()
        u.n, u.p, u.w, u.pf, u.ps = n, p, w, pf, ps
        u.first = (lambda j: at(dx=j % 4)) if n == 0 else (lambda j: at(dy=j % 4))
        u.second = (lambda j: at(dy=j % 4)) if n == 0 else (lambda j: at(dx=j % 4))
        u.r1, u.t1, u.s1, u.r2 = r1.at[n], t1.at[n], s1.at[n], r2.at[n]
        u.sem = lambda i, n=n: (xs.at[n, i], xr.at[n, i])
        units.append(u)

    def stage1(u):
        q2, qr, ql = (u.pf + 2) % 4, (u.pf + 1) % 4, (u.pf + 3) % 4
        u.a = [None] * 6
        u.a[0] = send(rows(u.p, q2 * BLK, HB), u.r1.at[0], *u.sem(0), u.first(1))
        u.a[3] = send(rows(u.p, q2 * BLK + HB, HB), u.r1.at[3], *u.sem(3), u.first(3))
        u.a[1] = send(rows(u.p, qr * BLK + HB, HB), u.r1.at[1], *u.sem(1), u.first(1))
        u.a[4] = send(rows(u.p, ql * BLK, HB), u.r1.at[4], *u.sem(4), u.first(3))

    def stage2(u):
        qr, ql = (u.pf + 1) % 4, (u.pf + 3) % 4
        u.a[0].wait_recv()
        u.t1[0] = (load(u.p, qr * BLK, HB) + u.r1[0].astype(F32)).astype(BF16)
        u.a[2] = send(u.t1.at[0], u.r1.at[2], *u.sem(2), u.first(1))
        u.a[3].wait_recv()
        u.t1[1] = (load(u.p, ql * BLK + HB, HB) + u.r1[3].astype(F32)).astype(BF16)
        u.a[5] = send(u.t1.at[1], u.r1.at[5], *u.sem(5), u.first(3))

    def stage3(u):
        for i in (1, 4, 2, 5):
            u.a[i].wait_recv()
        low = load(u.p, u.pf * BLK, HB) + u.r1[2].astype(F32) + u.r1[4].astype(F32)
        u.s1[0:HB, :] = low.astype(BF16)
        high = load(u.p, u.pf * BLK + HB, HB) + u.r1[1].astype(F32) + u.r1[5].astype(F32)
        u.s1[HB:BLK, :] = high.astype(BF16)
        u.b = [
            send(rows(u.s1, ((u.ps + j) % 4) * ROWS, ROWS), u.r2.at[j - 1], *u.sem(5 + j), u.second(j))
            for j in (1, 2, 3)
        ]

    def stage4(u):
        for copy in u.b:
            copy.wait_recv()
        total = load(u.s1, u.ps * ROWS, ROWS)
        for j in range(3):
            total = total + u.r2[j].astype(F32)
        total = total * wrow[:, u.n * HALF : (u.n + 1) * HALF]
        mine = u.pf * BLK + u.ps * ROWS
        u.w[pl.ds(pl.multiple_of(mine, 16), ROWS), :] = total.astype(BF16)
        u.c = [
            send(rows(u.w, mine, ROWS), rows(u.w, mine, ROWS), *u.sem(8 + j), u.second(j))
            for j in (1, 2, 3)
        ]

    def stage5(u):
        for copy in u.c:
            copy.wait_recv()
        low, high = rows(u.w, u.pf * BLK, HB), rows(u.w, u.pf * BLK + HB, HB)
        u.d = [None] * 6
        u.d[0] = send(low, low, *u.sem(12), u.first(1))
        u.d[3] = send(high, high, *u.sem(15), u.first(3))
        u.d[1] = send(high, high, *u.sem(13), u.first(1))
        u.d[4] = send(low, low, *u.sem(16), u.first(3))

    def stage6(u):
        u.d[0].wait_recv()
        low = rows(u.w, ((u.pf + 3) % 4) * BLK, HB)
        u.d[2] = send(low, low, *u.sem(14), u.first(1))
        u.d[3].wait_recv()
        high = rows(u.w, ((u.pf + 1) % 4) * BLK + HB, HB)
        u.d[5] = send(high, high, *u.sem(17), u.first(3))

    def stage7(u):
        for i in (1, 4, 2, 5):
            u.d[i].wait_recv()

    for u in units:
        stage1(u)

    f_codes.wait()
    f_ids.wait()
    weights = jnp.where(ids_v[...] == PAD, 0.0, jnp.exp(TEMP * codes_v[...].astype(F32)))
    for i in range(TOK // 128):
        wrow[:, i * 128 : (i + 1) * 128] = jnp.broadcast_to(weights[i : i + 1, :], (ROWS, 128))
    local = jnp.sum(jnp.sum(weights, axis=0, keepdims=True), axis=1, keepdims=True)
    nsend[0] = jnp.broadcast_to(local, (8, 128))
    ncore = send(nsend.at[0], nrecv.at[7], nss.at[7], nrs.at[7], at(dc=1))

    for u in units:
        stage2(u)
    ncore.wait_recv()
    nsend[1] = nsend[0] + nrecv[7]
    sums = [
        send(nsend.at[1], nrecv.at[j - 1], nss.at[j - 1], nrs.at[j - 1], at(dz=j))
        for j in range(1, NZ)
    ]
    for u in units:
        stage3(u)

    for u in units:
        stage4(u)
    for u in units:
        stage5(u)
    for u in units:
        stage6(u)
    for copy in sums:
        copy.wait_recv()
    scale = nsend[1]
    for i in range(7):
        scale = scale + nrecv[i]
    scale = TOKENS / scale[0:1, 0:1]
    for copy in f_og:
        copy.wait()
    for u in units:
        stage7(u)

    x0, y0 = dp % NX, dp // NX
    in_row, in_col = y == y0, x == x0
    is_src = jnp.logical_and(in_row, in_col)
    parts = (pl.ds(0, D // 2), pl.ds(D // 2, D // 2))
    hop = ((lambda j: at(dx=j), lambda j: at(dy=j)), (lambda j: at(dy=j), lambda j: at(dx=j)))
    member = (in_row, in_col)

    def spread(h, level, src):
        copies = []
        for j in (1, 2, 3):
            i = h * 6 + level * 3 + j - 1
            copies.append(
                pltpu.make_async_remote_copy(
                    src_ref=src.at[parts[h]], dst_ref=own_v.at[parts[h]],
                    send_sem=bs.at[i], recv_sem=br.at[h],
                    device_id=hop[h][level](j), device_id_type=MESH,
                )
            )
        return copies

    def basis_first():
        @pl.when(is_src)
        def _():
            pltpu.make_async_copy(basis_v, own_v, bl).start()
            for h in (0, 1):
                for copy in spread(h, 0, basis_v):
                    copy.start()
            for h in (0, 1):
                for copy in spread(h, 1, basis_v):
                    copy.start()

    def basis_second():
        for h in (0, 1):
            @pl.when(jnp.logical_and(member[h], jnp.logical_not(is_src)))
            def _(h=h):
                copies = spread(h, 1, own_v)
                copies[0].wait_recv()
                for copy in copies:
                    copy.start()

    def basis_last():
        @pl.when(is_src)
        def _():
            pltpu.make_async_copy(basis_v, own_v, bl).wait()
            for h in (0, 1):
                for copy in spread(h, 0, basis_v):
                    copy.wait_send()

        for h in (0, 1):
            copies = spread(h, 1, own_v)

            @pl.when(jnp.logical_not(member[h]))
            def _(copies=copies):
                copies[0].wait_recv()

            @pl.when(member[h])
            def _(copies=copies):
                for copy in copies:
                    copy.wait_send()

    cs, cr, tx, rx, up = (cs0, cs1), (cr0, cr1), (tx0, tx1), (rx0, rx1), (u0, u1)
    exch = [[], []]

    def block_of(k, core):
        return (((z + k) % NZ) * 2 + core) * ROWS

    def raw_columns(h):
        for lo in range(CUT[h], CUT[h + 1], 256):
            raw[:, lo : lo + 256] = jnp.dot(
                wx[...], og_v[0:HALF, lo : lo + 256], preferred_element_type=F32
            ) + jnp.dot(wy[...], og_v[HALF:TOK, lo : lo + 256], preferred_element_type=F32)
        for n, (at_slot, count) in enumerate(PIECES):
            for k, slot in SLOT.items():
                if at_slot <= slot < at_slot + count:
                    cs[h][slot] = raw[
                        pl.ds(pl.multiple_of(block_of(k, 1 - c), 16), ROWS), CUT[h] : CUT[h + 1]
                    ].astype(BF16)
            span = pl.ds(at_slot, count)
            exch[h].append(
                send(cs[h].at[span], cr[h].at[span], ces.at[h, n], cer.at[h, n], at(dc=1))
            )

    def chip_sum(k, h):
        mine = raw[pl.ds(pl.multiple_of(block_of(k, c), 16), ROWS), CUT[h] : CUT[h + 1]]
        return mine + cr[h][SLOT[k]].astype(F32)

    reduced = [[], []]

    def reduce_sends(h, offsets):
        for k in offsets:
            tx[h][k - 1] = chip_sum(k, h).astype(BF16)
            reduced[h].append(
                send(tx[h].at[k - 1], rx[h].at[k - 1], zs.at[h, k - 1], zr.at[h, k - 1], at(dz=k))
            )

    basis_first()
    for h in (0, 1):
        raw_columns(h)
        exch[h][0].wait_recv()
        reduce_sends(h, (4, 3, 5))
        exch[h][1].wait_recv()
        reduce_sends(h, (2, 6))
        exch[h][2].wait_recv()
        reduce_sends(h, (1, 7))
    basis_second()

    bias1 = 1.0 - B1**ADAM_STEP
    bias2 = 1.0 - B2**ADAM_STEP
    f_m1.wait()
    f_m2.wait()

    forwards, gathered = {}, {}

    def forward(h, off):
        block = up[h].at[((z + off) % NZ) * 2 + c]
        forwards[h, off] = send(block, block, fs.at[h, off], fr.at[h, off], at(dc=1))

    for h in (0, 1):
        for copy in reduced[h]:
            copy.wait_recv()
        grad = chip_sum(0, h)
        for k in range(NZ - 1):
            grad = grad + rx[h][k].astype(F32)
        grad = grad * scale
        cols = slice(CUT[h], CUT[h + 1])
        first = B1 * m1_v[:, cols] + (1.0 - B1) * grad
        second = B2 * m2_v[:, cols] + (1.0 - B2) * grad * grad
        up[h][dp] = ((first / bias1) / (jnp.sqrt(second / bias2) + EPS)).astype(BF16)
        for k in (4, 3, 5, 2, 6, 1, 7):
            gathered[h, k] = send(
                up[h].at[dp], up[h].at[dp], gs.at[h, k], gr.at[h, k], at(dz=k)
            )
        forward(h, 0)
        nf_v[:, cols] = first
        ns_v[:, cols] = second
    for h in (0, 1):
        for k in (1, 7, 2, 6, 3, 5, 4):
            gathered[h, k].wait_recv()
            forward(h, NZ - k)
    basis_last()
    for h in (0, 1):
        for off in range(NZ):
            forwards[h, off].wait_recv()
    for copy in pending:
        copy.wait_send()


def final_kernel(nf_v, ns_v, own_v, u0, u1, nf_o, ns_o, wu_o, wu_v, osem):
    copies = [
        pltpu.make_async_copy(nf_v, nf_o, osem.at[0]),
        pltpu.make_async_copy(ns_v, ns_o, osem.at[1]),
    ]
    for copy in copies:
        copy.start()
    n = 2
    for h, u in enumerate((u0, u1)):
        for lo in range(0, WID[h], 256):
            cols = pl.ds(CUT[h] + lo, 256)
            wu_v[:, CUT[h] + lo : CUT[h] + lo + 256] = jnp.dot(
                own_v[...], u[:, :, lo : lo + 256].reshape(R, 256), preferred_element_type=F32
            ).astype(BF16)
            copies.append(pltpu.make_async_copy(wu_v.at[:, cols], wu_o.at[:, cols], osem.at[n]))
            copies[-1].start()
            n += 1
    for copy in copies:
        copy.wait()


def local(activations, out_grads, basis, first_moment, second_moment, reward_codes, token_ids):
    hbm = pl.BlockSpec(memory_space=pltpu.HBM)
    near = pl.BlockSpec(memory_space=pltpu.VMEM)
    vm = pltpu.VMEM
    dma = pltpu.SemaphoreType.DMA
    moments = jax.ShapeDtypeStruct((ROWS, FF), F32)
    states = pl.pallas_call(
        kernel,
        out_shape=(
            vm((ROWS, FF), F32),
            vm((ROWS, FF), F32),
            vm((D, R), BF16),
            vm((16, ROWS, WID[0]), BF16),
            vm((16, ROWS, WID[1]), BF16),
        ),
        in_specs=[hbm] * 7,
        out_specs=(near,) * 5,
        scratch_shapes=[
            vm((TOK, D), BF16), vm((TOK, FF), BF16), vm((D, R), BF16), vm((R, D), BF16),
            vm((ROWS, FF), F32), vm((ROWS, FF), F32),
            vm((TOK // 128, 128), jnp.int32), vm((TOK // 128, 128), jnp.int32),
            vm((ROWS, TOK), F32),
            vm((R, HALF), BF16), vm((R, HALF), BF16), vm((R, HALF), BF16), vm((R, HALF), BF16),
            vm((2, 6, HB, HALF), BF16), vm((2, 2, HB, HALF), BF16), vm((2, BLK, HALF), BF16),
            vm((2, 3, ROWS, HALF), BF16), vm((R, FF), F32),
            vm((2, 8, 128), F32), vm((8, 8, 128), F32),
            vm((8, ROWS, WID[0]), BF16), vm((8, ROWS, WID[1]), BF16),
            vm((8, ROWS, WID[0]), BF16), vm((8, ROWS, WID[1]), BF16),
            vm((8, ROWS, WID[0]), BF16), vm((8, ROWS, WID[1]), BF16),
            vm((8, ROWS, WID[0]), BF16), vm((8, ROWS, WID[1]), BF16),
            dma((13,)), dma((2, 18)), dma((2, 18)), dma((8,)), dma((8,)),
            dma((2, 3)), dma((2, 3)), dma((2, 8)), dma((2, 8)), dma((2, 8)), dma((2, 8)),
            dma((2, 8)), dma((2, 8)), dma((12,)), dma((2,)), dma,
        ],
        compiler_params=pltpu.CompilerParams(
            collective_id=0, has_side_effects=True, vmem_limit_bytes=55_260_000
        ),
        name="galore_step",
    )(
        activations, out_grads, basis, first_moment, second_moment,
        reward_codes.reshape(TOK // 128, 128), token_ids.reshape(TOK // 128, 128),
    )
    return pl.pallas_call(
        final_kernel,
        out_shape=(moments, moments, jax.ShapeDtypeStruct((D, FF), BF16)),
        in_specs=[near] * 5,
        out_specs=(hbm, hbm, hbm),
        scratch_shapes=[vm((D, FF), BF16), dma((9,))],
        compiler_params=pltpu.CompilerParams(vmem_limit_bytes=16 * 1024 * 1024),
        name="project_back",
    )(*states)


def solution(mesh):
    return jax.shard_map(
        local,
        mesh=mesh,
        in_specs=(
            P("dp", "tensor"),
            P("dp", "tensor"),
            P("tensor", None),
            P("dp", "tensor"),
            P("dp", "tensor"),
            P("dp"),
            P("dp"),
        ),
        out_specs=(P("dp", "tensor"), P("dp", "tensor"), P("dp", "tensor")),
        check_vma=False,
    )
```

```python
import jax
import jax.numpy as jnp
from jax import lax
from jax.experimental import pallas as pl
from jax.experimental.pallas import tpu as pltpu
from jax.sharding import PartitionSpec as P

ADAM_STEP = 100
PAD = 128004
TEMP = 0.2
B1 = 0.9
B2 = 0.999
EPS = 1e-8
MESH = pl.DeviceIdType.MESH
F32 = jnp.float32
BF16 = jnp.bfloat16

NX = NY = 4
NZ = 8
TOK = 2304
HALF = TOK // 2
D = 512
R = 256
FF = 1792
ROWS = 16
PARTS = 2
RP = R // PARTS
BLK = RP // NX
SIDE = FF // 2
TOKENS = TOK * 16
SLOT = {4: 0, 3: 1, 5: 2, 2: 3, 6: 4, 1: 5, 7: 6, 0: 7}
PIECES = ((0, 3), (3, 2), (5, 3))


def rows(ref, start, size):
    return ref.at[pl.ds(pl.multiple_of(start, 16), size)]


def load(ref, start, size):
    return ref[pl.ds(pl.multiple_of(start, 16), size), :].astype(F32)


def side_by_side(ref, n):
    top = pl.ds(n * 8, 8)
    return jnp.concatenate([ref[top, 0:SIDE], ref[top, SIDE:FF]], axis=0)


def kernel(
    act, og, basis, m1, m2, codes, ids, nf_v, ns_v, own_v, up,
    act_v, og_v, basis_v, basis_t, m1_v, m2_v, codes_v, ids_v, wrow,
    p, w, r1, s1, r2, raw, nsend, nrecv, cs, cr, tx, rx,
    lsem, xs, xr, nss, nrs, ces, cer, zs, zr, gs, gr, fs, fr, bs, br, bl,
):
    dp = lax.axis_index("dp")
    tn = lax.axis_index("tensor")
    z, c = dp // 2, dp % 2
    y, x = tn // NX, tn % NX

    def at(dx=0, dy=0, dz=0, dc=0):
        return (
            ((z + dz) % NZ) * 2 + (c + dc) % 2,
            ((y + dy) % NY) * NX + (x + dx) % NX,
        )

    partners = [at(dx=j) for j in (1, 2, 3)] + [at(dy=j) for j in (1, 2, 3)]
    partners += [at(dz=j) for j in range(1, NZ)] + [at(dc=1)]
    barrier = pltpu.get_barrier_semaphore()
    for other in partners:
        pl.semaphore_signal(barrier, inc=1, device_id=other, device_id_type=MESH)

    pending = []

    def send(src, dst, ssem, rsem, to):
        copy = pltpu.make_async_remote_copy(
            src_ref=src, dst_ref=dst, send_sem=ssem, recv_sem=rsem,
            device_id=to, device_id_type=MESH,
        )
        copy.start()
        pending.append(copy)
        return copy

    def fetch(src, dst, n):
        copy = pltpu.make_async_copy(src, dst, lsem.at[n])
        copy.start()
        return copy

    f_basis = fetch(basis, basis_v, 0)
    step = TOK // 6
    f_act = [
        fetch(act.at[pl.ds(i * step, step)], act_v.at[pl.ds(i * step, step)], 1 + i)
        for i in range(6)
    ]
    f_codes = fetch(codes, codes_v, 7)
    f_ids = fetch(ids, ids_v, 8)
    f_m1 = fetch(m1, m1_v, 9)
    f_m2 = fetch(m2, m2_v, 10)
    f_og = [
        fetch(og.at[pl.ds(i * HALF, HALF)], og_v.at[pl.ds(i * HALF, HALF)], 11 + i)
        for i in range(2)
    ]

    f_basis.wait()
    turned = basis_v[...].astype(F32).T.reshape(16, PARTS, 8, D)
    for n in range(PARTS):
        basis_t[n * RP : (n + 1) * RP, :] = turned[:, n].reshape(RP, D).astype(BF16)
    for i in range(6):
        f_act[i].wait()
        part = lax.dot_general(
            basis_t[...], act_v[i * step : (i + 1) * step, :],
            (((1,), (1,)), ((), ())), preferred_element_type=F32,
        ).astype(BF16)
        for n in range(PARTS):
            p[n, :, i * step : (i + 1) * step] = part[n * RP : (n + 1) * RP, :]

    pl.semaphore_wait(barrier, len(partners))

    class Unit:
        pass

    units = []
    along_x, along_y = (lambda j: at(dx=j)), (lambda j: at(dy=j))
    for n in range(2 * PARTS):
        u = Unit()
        u.cols = pl.ds((n % 2) * HALF, HALF)
        u.n, u.p, u.w = n, p.at[n // 2, :, u.cols], w.at[n // 2, :, u.cols]
        u.pf = x if n % 2 == 0 else y
        u.first, u.second = (along_x, along_y) if n % 2 == 0 else (along_y, along_x)
        u.r1, u.s1, u.r2 = r1.at[n], s1.at[n], r2.at[n]
        units.append(u)

    def scatter_start(u):
        u.a = [
            send(rows(u.p, ((u.pf + j) % 4) * BLK, BLK), u.r1.at[j - 1],
                 xs.at[u.n, j - 1], xr.at[u.n, j - 1], u.first(j))
            for j in (2, 1, 3)
        ]

    def exchange_start(u):
        total = load(u.p, u.pf * BLK, BLK)
        for copy in u.a:
            copy.wait_recv()
        for j in range(3):
            total = total + u.r1[j].astype(F32)
        u.s1[...] = total.astype(BF16)
        u.b = [
            send(u.s1, u.r2.at[j - 1], xs.at[u.n, 2 + j], xr.at[u.n, 2 + j], u.second(j))
            for j in (2, 1, 3)
        ]

    def gather_start(u):
        for copy in u.b:
            copy.wait_recv()
        mine = pl.ds(pl.multiple_of(u.pf * BLK, 16), BLK)
        for lo in range(0, BLK, ROWS):
            total = u.s1[lo : lo + ROWS, :].astype(F32)
            for j in range(3):
                total = total + u.r2[j, lo : lo + ROWS, :].astype(F32)
            total = total * wrow[:, u.cols]
            u.w[pl.ds(pl.multiple_of(u.pf * BLK + lo, 16), ROWS), :] = total.astype(BF16)
        u.c = [
            send(u.w.at[mine], u.w.at[mine], xs.at[u.n, 5 + j], xr.at[u.n, 5 + j], u.first(j))
            for j in (2, 1, 3)
        ]

    def gather_end(u):
        for copy in u.c:
            copy.wait_recv()

    def units_of(n):
        return units[2 * n : 2 * n + 2]

    for u in units:
        scatter_start(u)

    f_codes.wait()
    f_ids.wait()
    weights = jnp.where(ids_v[...] == PAD, 0.0, jnp.exp(TEMP * codes_v[...].astype(F32)))
    for i in range(TOK // 128):
        wrow[:, i * 128 : (i + 1) * 128] = jnp.broadcast_to(weights[i : i + 1, :], (ROWS, 128))
    local = jnp.sum(jnp.sum(weights, axis=0, keepdims=True), axis=1, keepdims=True)
    nsend[0] = jnp.broadcast_to(local, (8, 128))
    ncore = send(nsend.at[0], nrecv.at[7], nss.at[7], nrs.at[7], at(dc=1))

    for u in units_of(0):
        exchange_start(u)
    ncore.wait_recv()
    nsend[1] = nsend[0] + nrecv[7]
    sums = [
        send(nsend.at[1], nrecv.at[j - 1], nss.at[j - 1], nrs.at[j - 1], at(dz=j))
        for j in range(1, NZ)
    ]
    for u in units_of(1):
        exchange_start(u)
    for n in range(PARTS):
        for u in units_of(n):
            gather_start(u)
    for copy in sums:
        copy.wait_recv()
    scale = nsend[1]
    for i in range(7):
        scale = scale + nrecv[i]
    scale = TOKENS / scale[0:1, 0:1]
    for copy in f_og + [f_m1, f_m2]:
        copy.wait()

    x0, y0 = dp % NX, dp // NX
    in_row, in_col = y == y0, x == x0
    is_src = jnp.logical_and(in_row, in_col)
    parts = (pl.ds(0, D // 2), pl.ds(D // 2, D // 2))
    hop = ((lambda j: at(dx=j), lambda j: at(dy=j)), (lambda j: at(dy=j), lambda j: at(dx=j)))
    member = (in_row, in_col)

    def spread(h, level, src):
        copies = []
        for j in (1, 2, 3):
            i = h * 6 + level * 3 + j - 1
            copies.append(
                pltpu.make_async_remote_copy(
                    src_ref=src.at[parts[h]], dst_ref=own_v.at[parts[h]],
                    send_sem=bs.at[i], recv_sem=br.at[h],
                    device_id=hop[h][level](j), device_id_type=MESH,
                )
            )
        return copies

    def basis_first():
        @pl.when(is_src)
        def _():
            pltpu.make_async_copy(basis_v, own_v, bl).start()
            for h in (0, 1):
                for copy in spread(h, 0, basis_v):
                    copy.start()
            for h in (0, 1):
                for copy in spread(h, 1, basis_v):
                    copy.start()

    def basis_second():
        for h in (0, 1):
            @pl.when(jnp.logical_and(member[h], jnp.logical_not(is_src)))
            def _(h=h):
                copies = spread(h, 1, own_v)
                copies[0].wait_recv()
                for copy in copies:
                    copy.start()

    def basis_last():
        @pl.when(is_src)
        def _():
            pltpu.make_async_copy(basis_v, own_v, bl).wait()
            for h in (0, 1):
                for copy in spread(h, 0, basis_v):
                    copy.wait_send()

        for h in (0, 1):
            copies = spread(h, 1, own_v)

            @pl.when(jnp.logical_not(member[h]))
            def _(copies=copies):
                copies[0].wait_recv()

            @pl.when(member[h])
            def _(copies=copies):
                for copy in copies:
                    copy.wait_send()

    exch = [[], []]

    def owner(k, core):
        return ((z + k) % NZ) * 2 + core

    def multiply(n):
        for lo in range(0, FF, 128 * 7):
            for at_, width in ((0, 256), (256, 256), (512, 256), (768, 128)):
                part = jnp.dot(
                    w[n], og_v[:, lo + at_ : lo + at_ + width], preferred_element_type=F32
                )
                top = 0 if lo == 0 else 8
                raw[n, :, top : top + 8, at_ : at_ + width] = part.reshape(16, 8, width)
        for i, (at_slot, count) in enumerate(PIECES):
            for k, slot in SLOT.items():
                if at_slot <= slot < at_slot + count:
                    cs[n, slot] = raw[n, owner(k, 1 - c)].astype(BF16)
            span = pl.ds(at_slot, count)
            exch[n].append(
                send(cs.at[n, span], cr.at[n, span], ces.at[n, i], cer.at[n, i], at(dc=1))
            )

    def chip_sum(k, n):
        return raw[n, owner(k, c)] + cr[n, SLOT[k]].astype(F32)

    reduced = [[], []]

    def reduce_start(n):
        for i, offsets in enumerate(((4, 3, 5), (2, 6), (1, 7))):
            exch[n][i].wait_recv()
            for k in offsets:
                tx[n, k - 1] = chip_sum(k, n).astype(BF16)
                reduced[n].append(
                    send(tx.at[n, k - 1], rx.at[n, k - 1], zs.at[n, k - 1], zr.at[n, k - 1], at(dz=k))
                )

    bias1 = 1.0 - B1**ADAM_STEP
    bias2 = 1.0 - B2**ADAM_STEP
    forwards, gathered = {}, {}

    def forward(n, off):
        block = up.at[n, ((z + off) % NZ) * 2 + c]
        forwards[n, off] = send(block, block, fs.at[n, off], fr.at[n, off], at(dc=1))

    def adam(n):
        for copy in reduced[n]:
            copy.wait_recv()
        grad = chip_sum(0, n)
        for k in range(NZ - 1):
            grad = grad + rx[n, k].astype(F32)
        grad = grad * scale
        first = B1 * side_by_side(m1_v, n) + (1.0 - B1) * grad
        second = B2 * side_by_side(m2_v, n) + (1.0 - B2) * grad * grad
        up[n, dp] = ((first / bias1) / (jnp.sqrt(second / bias2) + EPS)).astype(BF16)
        block = up.at[n, dp]
        for k in (4, 3, 5, 2, 6, 1, 7):
            gathered[n, k] = send(block, block, gs.at[n, k], gr.at[n, k], at(dz=k))
        forward(n, 0)
        for ref, value in ((nf_v, first), (ns_v, second)):
            ref[n * 8 : n * 8 + 8, 0:SIDE] = value[0:8]
            ref[n * 8 : n * 8 + 8, SIDE:FF] = value[8:16]

    for n in range(PARTS):
        for u in units_of(n):
            gather_end(u)
        if n == PARTS - 1:
            basis_first()
        multiply(n)
        reduce_start(n)
    basis_second()
    for n in range(PARTS):
        adam(n)
    for n in range(PARTS):
        for k in (1, 7, 2, 6, 3, 5, 4):
            gathered[n, k].wait_recv()
            forward(n, NZ - k)
    basis_last()
    for n in range(PARTS):
        for off in range(NZ):
            forwards[n, off].wait_recv()
    for copy in pending:
        copy.wait_send()


def final_kernel(nf_v, ns_v, own_v, up, nf_o, ns_o, wu_o, wu_v, osem):
    copies = [
        pltpu.make_async_copy(nf_v, nf_o, osem.at[0]),
        pltpu.make_async_copy(ns_v, ns_o, osem.at[1]),
    ]
    for copy in copies:
        copy.start()
    n = 2
    for h in (0, 1):
        for at_, width in ((0, 256), (256, 256), (512, 256), (768, 128)):
            lines = [
                up[i, :, :, at_ : at_ + width].astype(F32)[:, h * 8 : h * 8 + 8] for i in range(PARTS)
            ]
            lines = jnp.concatenate(lines, axis=1).astype(BF16).reshape(R, width)
            lo = h * SIDE + at_
            cols = pl.ds(lo, width)
            wu_v[:, lo : lo + width] = jnp.dot(
                own_v[...], lines, preferred_element_type=F32
            ).astype(BF16)
            copies.append(pltpu.make_async_copy(wu_v.at[:, cols], wu_o.at[:, cols], osem.at[n]))
            copies[-1].start()
            n += 1
    for copy in copies:
        copy.wait()


def local(activations, out_grads, basis, first_moment, second_moment, reward_codes, token_ids):
    hbm = pl.BlockSpec(memory_space=pltpu.HBM)
    near = pl.BlockSpec(memory_space=pltpu.VMEM)
    vm = pltpu.VMEM
    dma = pltpu.SemaphoreType.DMA
    moments = jax.ShapeDtypeStruct((ROWS, FF), F32)
    states = pl.pallas_call(
        kernel,
        out_shape=(
            vm((ROWS, FF), F32),
            vm((ROWS, FF), F32),
            vm((D, R), BF16),
            vm((PARTS, 16, ROWS, SIDE), BF16),
        ),
        in_specs=[hbm] * 7,
        out_specs=(near,) * 4,
        scratch_shapes=[
            vm((TOK, D), BF16), vm((TOK, FF), BF16), vm((D, R), BF16), vm((R, D), BF16),
            vm((ROWS, FF), F32), vm((ROWS, FF), F32),
            vm((TOK // 128, 128), jnp.int32), vm((TOK // 128, 128), jnp.int32),
            vm((ROWS, TOK), F32),
            vm((PARTS, RP, TOK), BF16), vm((PARTS, RP, TOK), BF16),
            vm((2 * PARTS, 3, BLK, HALF), BF16), vm((2 * PARTS, BLK, HALF), BF16),
            vm((2 * PARTS, 3, BLK, HALF), BF16), vm((PARTS, 16, ROWS, SIDE), F32),
            vm((2, 8, 128), F32), vm((8, 8, 128), F32),
            vm((PARTS, 8, ROWS, SIDE), BF16), vm((PARTS, 8, ROWS, SIDE), BF16),
            vm((PARTS, 8, ROWS, SIDE), BF16), vm((PARTS, 8, ROWS, SIDE), BF16),
            dma((13,)), dma((2 * PARTS, 9)), dma((2 * PARTS, 9)), dma((8,)), dma((8,)),
            dma((2, 3)), dma((2, 3)), dma((2, 8)), dma((2, 8)), dma((2, 8)), dma((2, 8)),
            dma((2, 8)), dma((2, 8)), dma((12,)), dma((2,)), dma,
        ],
        compiler_params=pltpu.CompilerParams(
            collective_id=0, has_side_effects=True, vmem_limit_bytes=55_260_000
        ),
        name="galore_step",
    )(
        activations, out_grads, basis, first_moment, second_moment,
        reward_codes.reshape(TOK // 128, 128), token_ids.reshape(TOK // 128, 128),
    )
    return pl.pallas_call(
        final_kernel,
        out_shape=(moments, moments, jax.ShapeDtypeStruct((D, FF), BF16)),
        in_specs=[near] * 4,
        out_specs=(hbm, hbm, hbm),
        scratch_shapes=[vm((D, FF), BF16), dma((10,))],
        compiler_params=pltpu.CompilerParams(vmem_limit_bytes=16 * 1024 * 1024),
        name="project_back",
    )(*states)


def solution(mesh):
    return jax.shard_map(
        local,
        mesh=mesh,
        in_specs=(
            P("dp", "tensor"),
            P("dp", "tensor"),
            P("tensor", None),
            P("dp", "tensor"),
            P("dp", "tensor"),
            P("dp"),
            P("dp"),
        ),
        out_specs=(P("dp", "tensor"), P("dp", "tensor"), P("dp", "tensor")),
        check_vma=False,
    )
```

```python
import jax
import jax.numpy as jnp
from jax import lax
from jax.experimental import pallas as pl
from jax.experimental.pallas import tpu as pltpu
from jax.sharding import PartitionSpec as P

ADAM_STEP = 100
PAD = 128004
TEMP = 0.2
B1 = 0.9
B2 = 0.999
EPS = 1e-8
MESH = pl.DeviceIdType.MESH
F32 = jnp.float32
BF16 = jnp.bfloat16

NX = NY = 4
NZ = 8
TOK = 2304
HALF = TOK // 2
D = 512
R = 256
FF = 1792
ROWS = 16
PARTS = 2
RP = R // PARTS
BLK = RP // NX
SIDE = FF // 2
TOKENS = TOK * 16
SLOT = {4: 0, 3: 1, 5: 2, 2: 3, 6: 4, 1: 5, 7: 6, 0: 7}
LEFT, RIGHT = pl.ds(0, 512), pl.ds(512, SIDE - 512)
SUM_RELAY = (0, 1)
GATHER_RELAY = (0, 1)
PIECES = ((0, 3), (3, 2), (5, 3))


def rows(ref, start, size):
    return ref.at[pl.ds(pl.multiple_of(start, 16), size)]


def load(ref, start, size):
    return ref[pl.ds(pl.multiple_of(start, 16), size), :].astype(F32)


def side_by_side(ref, n):
    top = pl.ds(n * 8, 8)
    return jnp.concatenate([ref[top, 0:SIDE], ref[top, SIDE:FF]], axis=0)


def kernel(
    act, og, basis, m1, m2, codes, ids, nf_v, ns_v, own_v, up,
    act_v, og_v, basis_v, basis_t, m1_v, m2_v, codes_v, ids_v, wrow,
    p, w, r1, s1, r2, raw, nsend, nrecv, cs, cr, tx, rx,
    lsem, xs, xr, nss, nrs, ces, cer, zs, zr, gs, gr, fs, fr, bs, br, bl,
):
    dp = lax.axis_index("dp")
    tn = lax.axis_index("tensor")
    z, c = dp // 2, dp % 2
    y, x = tn // NX, tn % NX

    def at(dx=0, dy=0, dz=0, dc=0):
        return (
            ((z + dz) % NZ) * 2 + (c + dc) % 2,
            ((y + dy) % NY) * NX + (x + dx) % NX,
        )

    partners = [at(dx=j) for j in (1, 2, 3)] + [at(dy=j) for j in (1, 2, 3)]
    partners += [at(dz=j) for j in range(1, NZ)] + [at(dc=1)]
    barrier = pltpu.get_barrier_semaphore()
    for other in partners:
        pl.semaphore_signal(barrier, inc=1, device_id=other, device_id_type=MESH)

    pending = []

    def send(src, dst, ssem, rsem, to):
        copy = pltpu.make_async_remote_copy(
            src_ref=src, dst_ref=dst, send_sem=ssem, recv_sem=rsem,
            device_id=to, device_id_type=MESH,
        )
        copy.start()
        pending.append(copy)
        return copy

    def fetch(src, dst, n):
        copy = pltpu.make_async_copy(src, dst, lsem.at[n])
        copy.start()
        return copy

    f_basis = fetch(basis, basis_v, 0)
    step = TOK // 6
    f_act = [
        fetch(act.at[pl.ds(i * step, step)], act_v.at[pl.ds(i * step, step)], 1 + i)
        for i in range(6)
    ]
    f_codes = fetch(codes, codes_v, 7)
    f_ids = fetch(ids, ids_v, 8)
    f_m1 = fetch(m1, m1_v, 9)
    f_m2 = fetch(m2, m2_v, 10)
    f_og = [
        fetch(og.at[pl.ds(i * HALF, HALF)], og_v.at[pl.ds(i * HALF, HALF)], 11 + i)
        for i in range(2)
    ]

    f_basis.wait()
    turned = basis_v[...].astype(F32).T.reshape(16, PARTS, 8, D)
    for n in range(PARTS):
        basis_t[n * RP : (n + 1) * RP, :] = turned[:, n].reshape(RP, D).astype(BF16)
    for copy in f_act:
        copy.wait()

    def project(n):
        for i in range(6):
            p[n, :, i * step : (i + 1) * step] = lax.dot_general(
                basis_t[n * RP : (n + 1) * RP, :], act_v[i * step : (i + 1) * step, :],
                (((1,), (1,)), ((), ())), preferred_element_type=F32,
            ).astype(BF16)

    project(0)
    pl.semaphore_wait(barrier, len(partners))

    class Unit:
        pass

    units = []
    along_x, along_y = (lambda j: at(dx=j)), (lambda j: at(dy=j))
    for n in range(2 * PARTS):
        u = Unit()
        u.cols = pl.ds((n % 2) * HALF, HALF)
        u.n, u.p, u.w = n, p.at[n // 2, :, u.cols], w.at[n // 2, :, u.cols]
        u.pf = x if n % 2 == 0 else y
        u.first, u.second = (along_x, along_y) if n % 2 == 0 else (along_y, along_x)
        u.r1, u.s1, u.r2 = r1.at[n], s1.at[n], r2.at[n]
        units.append(u)

    def scatter_start(u):
        u.a = [
            send(rows(u.p, ((u.pf + j) % 4) * BLK, BLK), u.r1.at[j - 1],
                 xs.at[u.n, j - 1], xr.at[u.n, j - 1], u.first(j))
            for j in (2, 1, 3)
        ]

    def exchange_start(u):
        total = load(u.p, u.pf * BLK, BLK)
        for copy in u.a:
            copy.wait_recv()
        for j in range(3):
            total = total + u.r1[j].astype(F32)
        u.s1[...] = total.astype(BF16)
        u.b = [
            send(u.s1, u.r2.at[j - 1], xs.at[u.n, 2 + j], xr.at[u.n, 2 + j], u.second(j))
            for j in (2, 1, 3)
        ]

    def gather_start(u):
        for copy in u.b:
            copy.wait_recv()
        mine = pl.ds(pl.multiple_of(u.pf * BLK, 16), BLK)
        for lo in range(0, BLK, ROWS):
            total = u.s1[lo : lo + ROWS, :].astype(F32)
            for j in range(3):
                total = total + u.r2[j, lo : lo + ROWS, :].astype(F32)
            total = total * wrow[:, u.cols]
            u.w[pl.ds(pl.multiple_of(u.pf * BLK + lo, 16), ROWS), :] = total.astype(BF16)
        u.c = [
            send(u.w.at[mine], u.w.at[mine], xs.at[u.n, 5 + j], xr.at[u.n, 5 + j], u.first(j))
            for j in (2, 1, 3)
        ]

    def gather_end(u):
        for copy in u.c:
            copy.wait_recv()

    def units_of(n):
        return units[2 * n : 2 * n + 2]

    for u in units_of(0):
        scatter_start(u)
    project(1)
    for u in units_of(1):
        scatter_start(u)

    f_codes.wait()
    f_ids.wait()
    weights = jnp.where(ids_v[...] == PAD, 0.0, jnp.exp(TEMP * codes_v[...].astype(F32)))
    for i in range(TOK // 128):
        wrow[:, i * 128 : (i + 1) * 128] = jnp.broadcast_to(weights[i : i + 1, :], (ROWS, 128))
    local = jnp.sum(jnp.sum(weights, axis=0, keepdims=True), axis=1, keepdims=True)
    nsend[0] = jnp.broadcast_to(local, (8, 128))
    ncore = send(nsend.at[0], nrecv.at[7], nss.at[7], nrs.at[7], at(dc=1))

    for u in units_of(0):
        exchange_start(u)
    ncore.wait_recv()
    nsend[1] = nsend[0] + nrecv[7]
    sums = [
        send(nsend.at[1], nrecv.at[j - 1], nss.at[j - 1], nrs.at[j - 1], at(dz=j))
        for j in range(1, NZ)
    ]
    for u in units_of(1):
        exchange_start(u)
    for n in range(PARTS):
        for u in units_of(n):
            gather_start(u)
    for copy in sums:
        copy.wait_recv()
    scale = nsend[1]
    for i in range(7):
        scale = scale + nrecv[i]
    scale = TOKENS / scale[0:1, 0:1]
    for copy in f_og + [f_m1, f_m2]:
        copy.wait()

    x0, y0 = dp % NX, dp // NX
    in_row, in_col = y == y0, x == x0
    is_src = jnp.logical_and(in_row, in_col)
    parts = (pl.ds(0, D // 2), pl.ds(D // 2, D // 2))
    hop = ((lambda j: at(dx=j), lambda j: at(dy=j)), (lambda j: at(dy=j), lambda j: at(dx=j)))
    member = (in_row, in_col)

    def spread(h, level, src):
        copies = []
        for j in (1, 2, 3):
            i = h * 6 + level * 3 + j - 1
            copies.append(
                pltpu.make_async_remote_copy(
                    src_ref=src.at[parts[h]], dst_ref=own_v.at[parts[h]],
                    send_sem=bs.at[i], recv_sem=br.at[h],
                    device_id=hop[h][level](j), device_id_type=MESH,
                )
            )
        return copies

    def basis_first():
        @pl.when(is_src)
        def _():
            pltpu.make_async_copy(basis_v, own_v, bl).start()
            for h in (0, 1):
                for copy in spread(h, 0, basis_v):
                    copy.start()
            for h in (0, 1):
                for copy in spread(h, 1, basis_v):
                    copy.start()

    def basis_second():
        for h in (0, 1):
            @pl.when(jnp.logical_and(member[h], jnp.logical_not(is_src)))
            def _(h=h):
                copies = spread(h, 1, own_v)
                copies[0].wait_recv()
                for copy in copies:
                    copy.start()

    def basis_last():
        @pl.when(is_src)
        def _():
            pltpu.make_async_copy(basis_v, own_v, bl).wait()
            for h in (0, 1):
                for copy in spread(h, 0, basis_v):
                    copy.wait_send()

        for h in (0, 1):
            copies = spread(h, 1, own_v)

            @pl.when(jnp.logical_not(member[h]))
            def _(copies=copies):
                copies[0].wait_recv()

            @pl.when(member[h])
            def _(copies=copies):
                for copy in copies:
                    copy.wait_send()

    exch = [[], []]

    def owner(k, core):
        return ((z + k) % NZ) * 2 + core

    def multiply(n):
        for lo in range(0, FF, 128 * 7):
            for at_, width in ((0, 256), (256, 256), (512, 256), (768, 128)):
                part = jnp.dot(
                    w[n], og_v[:, lo + at_ : lo + at_ + width], preferred_element_type=F32
                )
                top = 0 if lo == 0 else 8
                raw[n, :, top : top + 8, at_ : at_ + width] = part.reshape(16, 8, width)
        for i, (at_slot, count) in enumerate(PIECES):
            for k, slot in SLOT.items():
                if at_slot <= slot < at_slot + count:
                    cs[n, slot] = raw[n, owner(k, 1 - c)].astype(BF16)
            span = pl.ds(at_slot, count)
            exch[n].append(
                send(cs.at[n, span], cr.at[n, span], ces.at[n, i], cer.at[n, i], at(dc=1))
            )

    def chip_sum(k, n):
        return raw[n, owner(k, c)] + cr[n, SLOT[k]].astype(F32)

    reduced = [[], []]

    def reduce_send(n, k, to, sem, cols=slice(None)):
        return send(
            tx.at[n, k - 1, :, cols], rx.at[n, k - 1, :, cols], zs.at[n, sem], zr.at[n, sem], at(dz=to)
        )

    relayed = {}

    def reduce_start_relayed(n):
        exch[n][0].wait_recv()
        for k in (4, 3, 5):
            tx[n, k - 1] = chip_sum(k, n).astype(BF16)
            if k == 4:
                relayed[n, "a"] = reduce_send(n, 4, 2, 3, LEFT)
                relayed[n, "b"] = reduce_send(n, 4, 6, 7, RIGHT)
            else:
                relayed[n, k] = reduce_send(n, k, 1 if k == 3 else 7, k - 1)
        exch[n][1].wait_recv()
        exch[n][2].wait_recv()
        for k in (1, 7):
            tx[n, k - 1] = chip_sum(k, n).astype(BF16)
            reduced[n].append(reduce_send(n, k, k, k - 1))

    def reduce_relay(n):
        for k, near, far, cols in ((2, 3, "a", LEFT), (6, 5, "b", RIGHT)):
            relayed[n, near].wait_recv()
            relayed[n, far].wait_recv()
            total = chip_sum(k, n) + rx[n, near - 1].astype(F32)
            tx[n, k - 1] = total.astype(BF16)
            more = total[:, cols.start : cols.start + cols.size] + rx[n, 3, :, cols].astype(F32)
            tx[n, k - 1, :, cols] = more.astype(BF16)
            reduced[n].append(reduce_send(n, k, k, k - 1))

    def reduce_start(n):
        for i, offsets in enumerate(((4, 3, 5), (2, 6), (1, 7))):
            exch[n][i].wait_recv()
            for k in offsets:
                tx[n, k - 1] = chip_sum(k, n).astype(BF16)
                reduced[n].append(
                    send(tx.at[n, k - 1], rx.at[n, k - 1], zs.at[n, k - 1], zr.at[n, k - 1], at(dz=k))
                )

    bias1 = 1.0 - B1**ADAM_STEP
    bias2 = 1.0 - B2**ADAM_STEP
    forwards, gathered = {}, {}

    def forward(n, off):
        block = up.at[n, ((z + off) % NZ) * 2 + c]
        forwards[n, off] = send(block, block, fs.at[n, off], fr.at[n, off], at(dc=1))

    def gather_relay(n):
        for k, near, half, cols in ((2, 3, 4, LEFT), (6, 5, 0, RIGHT)):
            gathered[n, k].wait_recv()
            block = up.at[n, ((z + NZ - k) % NZ) * 2 + c]
            part = up.at[n, ((z + NZ - k) % NZ) * 2 + c, :, cols]
            gathered[n, half] = send(part, part, gs.at[n, half], gr.at[n, half], at(dz=k))
            gathered[n, near] = send(
                block, block, gs.at[n, near], gr.at[n, near], at(dz=1 if k == 2 else NZ - 1)
            )

    def adam(n):
        for copy in reduced[n]:
            copy.wait_recv()
        grad = chip_sum(0, n)
        for k in (0, 1, 5, 6) if n in SUM_RELAY else range(NZ - 1):
            grad = grad + rx[n, k].astype(F32)
        grad = grad * scale
        first = B1 * side_by_side(m1_v, n) + (1.0 - B1) * grad
        second = B2 * side_by_side(m2_v, n) + (1.0 - B2) * grad * grad
        up[n, dp] = ((first / bias1) / (jnp.sqrt(second / bias2) + EPS)).astype(BF16)
        block = up.at[n, dp]
        for k in (2, 6, 1, 7) if n in GATHER_RELAY else (4, 3, 5, 2, 6, 1, 7):
            gathered[n, k] = send(block, block, gs.at[n, k], gr.at[n, k], at(dz=k))
        forward(n, 0)
        for ref, value in ((nf_v, first), (ns_v, second)):
            ref[n * 8 : n * 8 + 8, 0:SIDE] = value[0:8]
            ref[n * 8 : n * 8 + 8, SIDE:FF] = value[8:16]

    for n in range(PARTS):
        for u in units_of(n):
            gather_end(u)
        multiply(n)
        if n in SUM_RELAY:
            reduce_start_relayed(n)
        else:
            reduce_start(n)
    basis_first()
    for n in range(PARTS):
        if n in SUM_RELAY:
            reduce_relay(n)
    for n in range(PARTS):
        adam(n)
    basis_second()
    for n in range(PARTS):
        if n in GATHER_RELAY:
            gather_relay(n)
    for n in range(PARTS):
        if n in GATHER_RELAY:
            for k in (1, 7):
                gathered[n, k].wait_recv()
                forward(n, NZ - k)
            for k in (2, 6):
                forward(n, NZ - k)
            for k in (3, 5):
                gathered[n, k].wait_recv()
                forward(n, NZ - k)
            gathered[n, 4].wait_recv()
            gathered[n, 0].wait_recv()
            forward(n, 4)
        else:
            for k in (1, 7, 2, 6, 3, 5, 4):
                gathered[n, k].wait_recv()
                forward(n, NZ - k)
    basis_last()
    for n in range(PARTS):
        for off in range(NZ):
            forwards[n, off].wait_recv()
    for copy in pending:
        copy.wait_send()


def final_kernel(nf_v, ns_v, own_v, up, nf_o, ns_o, wu_o, wu_v, osem):
    copies = [
        pltpu.make_async_copy(nf_v, nf_o, osem.at[0]),
        pltpu.make_async_copy(ns_v, ns_o, osem.at[1]),
    ]
    for copy in copies:
        copy.start()
    n = 2
    for h in (0, 1):
        for at_, width in ((0, 256), (256, 256), (512, 256), (768, 128)):
            lines = [
                up[i, :, :, at_ : at_ + width].astype(F32)[:, h * 8 : h * 8 + 8] for i in range(PARTS)
            ]
            lines = jnp.concatenate(lines, axis=1).astype(BF16).reshape(R, width)
            lo = h * SIDE + at_
            cols = pl.ds(lo, width)
            wu_v[:, lo : lo + width] = jnp.dot(
                own_v[...], lines, preferred_element_type=F32
            ).astype(BF16)
            copies.append(pltpu.make_async_copy(wu_v.at[:, cols], wu_o.at[:, cols], osem.at[n]))
            copies[-1].start()
            n += 1
    for copy in copies:
        copy.wait()


def local(activations, out_grads, basis, first_moment, second_moment, reward_codes, token_ids):
    hbm = pl.BlockSpec(memory_space=pltpu.HBM)
    near = pl.BlockSpec(memory_space=pltpu.VMEM)
    vm = pltpu.VMEM
    dma = pltpu.SemaphoreType.DMA
    moments = jax.ShapeDtypeStruct((ROWS, FF), F32)
    states = pl.pallas_call(
        kernel,
        out_shape=(
            vm((ROWS, FF), F32),
            vm((ROWS, FF), F32),
            vm((D, R), BF16),
            vm((PARTS, 16, ROWS, SIDE), BF16),
        ),
        in_specs=[hbm] * 7,
        out_specs=(near,) * 4,
        scratch_shapes=[
            vm((TOK, D), BF16), vm((TOK, FF), BF16), vm((D, R), BF16), vm((R, D), BF16),
            vm((ROWS, FF), F32), vm((ROWS, FF), F32),
            vm((TOK // 128, 128), jnp.int32), vm((TOK // 128, 128), jnp.int32),
            vm((ROWS, TOK), F32),
            vm((PARTS, RP, TOK), BF16), vm((PARTS, RP, TOK), BF16),
            vm((2 * PARTS, 3, BLK, HALF), BF16), vm((2 * PARTS, BLK, HALF), BF16),
            vm((2 * PARTS, 3, BLK, HALF), BF16), vm((PARTS, 16, ROWS, SIDE), F32),
            vm((2, 8, 128), F32), vm((8, 8, 128), F32),
            vm((PARTS, 8, ROWS, SIDE), BF16), vm((PARTS, 8, ROWS, SIDE), BF16),
            vm((PARTS, 8, ROWS, SIDE), BF16), vm((PARTS, 8, ROWS, SIDE), BF16),
            dma((13,)), dma((2 * PARTS, 9)), dma((2 * PARTS, 9)), dma((8,)), dma((8,)),
            dma((2, 3)), dma((2, 3)), dma((2, 8)), dma((2, 8)), dma((2, 8)), dma((2, 8)),
            dma((2, 8)), dma((2, 8)), dma((12,)), dma((2,)), dma,
        ],
        compiler_params=pltpu.CompilerParams(
            collective_id=0, has_side_effects=True, vmem_limit_bytes=55_260_000
        ),
        name="galore_step",
    )(
        activations, out_grads, basis, first_moment, second_moment,
        reward_codes.reshape(TOK // 128, 128), token_ids.reshape(TOK // 128, 128),
    )
    return pl.pallas_call(
        final_kernel,
        out_shape=(moments, moments, jax.ShapeDtypeStruct((D, FF), BF16)),
        in_specs=[near] * 4,
        out_specs=(hbm, hbm, hbm),
        scratch_shapes=[vm((D, FF), BF16), dma((10,))],
        compiler_params=pltpu.CompilerParams(vmem_limit_bytes=16 * 1024 * 1024),
        name="project_back",
    )(*states)


def solution(mesh):
    return jax.shard_map(
        local,
        mesh=mesh,
        in_specs=(
            P("dp", "tensor"),
            P("dp", "tensor"),
            P("tensor", None),
            P("dp", "tensor"),
            P("dp", "tensor"),
            P("dp"),
            P("dp"),
        ),
        out_specs=(P("dp", "tensor"), P("dp", "tensor"), P("dp", "tensor")),
        check_vma=False,
    )
```

```python
import jax
import jax.numpy as jnp
from jax import lax
from jax.experimental import pallas as pl
from jax.experimental.pallas import tpu as pltpu
from jax.sharding import PartitionSpec as P

ADAM_STEP = 100
PAD = 128004
TEMP = 0.2
B1 = 0.9
B2 = 0.999
EPS = 1e-8
MESH = pl.DeviceIdType.MESH
F32 = jnp.float32
BF16 = jnp.bfloat16

NX = NY = 4
NZ = 8
TOK = 2304
HALF = TOK // 2
D = 512
R = 256
FF = 1792
ROWS = 16
PARTS = 2
RP = R // PARTS
BLK = RP // NX
SIDE = FF // 2
TOKENS = TOK * 16
SLOT = {4: 0, 3: 1, 5: 2, 2: 3, 6: 4, 1: 5, 7: 6, 0: 7}
LEFT, RIGHT = pl.ds(0, 512), pl.ds(512, SIDE - 512)
SUM_RELAY = (0, 1)
GATHER_RELAY = (0, 1)
PIECES = ((0, 3), (3, 2), (5, 3))


def rows(ref, start, size):
    return ref.at[pl.ds(pl.multiple_of(start, 16), size)]


def load(ref, start, size):
    return ref[pl.ds(pl.multiple_of(start, 16), size), :].astype(F32)


def side_by_side(ref, n):
    top = pl.ds(n * 8, 8)
    return jnp.concatenate([ref[top, 0:SIDE], ref[top, SIDE:FF]], axis=0)


def kernel(
    act, og, basis, m1, m2, codes, ids, nf_v, ns_v, own_v, up,
    act_v, og_v, basis_v, basis_t, m1_v, m2_v, codes_v, ids_v, wrow,
    p, w, r1, s1, r2, raw, nsend, nrecv, cs, cr, tx, rx,
    lsem, xs, xr, nss, nrs, ces, cer, zs, zr, gs, gr, fs, fr, bs, br, bl,
):
    dp = lax.axis_index("dp")
    tn = lax.axis_index("tensor")
    z, c = dp // 2, dp % 2
    y, x = tn // NX, tn % NX

    def at(dx=0, dy=0, dz=0, dc=0):
        return (
            ((z + dz) % NZ) * 2 + (c + dc) % 2,
            ((y + dy) % NY) * NX + (x + dx) % NX,
        )

    partners = [at(dx=j) for j in (1, 2, 3)] + [at(dy=j) for j in (1, 2, 3)]
    partners += [at(dz=j) for j in range(1, NZ)] + [at(dc=1)]
    barrier = pltpu.get_barrier_semaphore()
    for other in partners:
        pl.semaphore_signal(barrier, inc=1, device_id=other, device_id_type=MESH)

    pending = []

    def send(src, dst, ssem, rsem, to):
        copy = pltpu.make_async_remote_copy(
            src_ref=src, dst_ref=dst, send_sem=ssem, recv_sem=rsem,
            device_id=to, device_id_type=MESH,
        )
        copy.start()
        pending.append(copy)
        return copy

    def drain(count):
        for copy in pending[:count]:
            copy.wait_send()
        del pending[:count]

    def fetch(src, dst, n):
        copy = pltpu.make_async_copy(src, dst, lsem.at[n])
        copy.start()
        return copy

    f_basis = fetch(basis, basis_v, 0)
    step = TOK // 6
    f_act = [
        fetch(act.at[pl.ds(i * step, step)], act_v.at[pl.ds(i * step, step)], 1 + i)
        for i in range(6)
    ]
    f_codes = fetch(codes, codes_v, 7)
    f_ids = fetch(ids, ids_v, 8)
    f_m1 = fetch(m1, m1_v, 9)
    f_m2 = fetch(m2, m2_v, 10)
    f_og = [
        fetch(og.at[pl.ds(i * HALF, HALF)], og_v.at[pl.ds(i * HALF, HALF)], 11 + i)
        for i in range(2)
    ]

    f_basis.wait()
    turned = basis_v[...].astype(F32).T.reshape(16, PARTS, 8, D)
    for n in range(PARTS):
        basis_t[n * RP : (n + 1) * RP, :] = turned[:, n].reshape(RP, D).astype(BF16)
    for copy in f_act:
        copy.wait()

    def project(n):
        for i in range(6):
            p[n, :, i * step : (i + 1) * step] = lax.dot_general(
                basis_t[n * RP : (n + 1) * RP, :], act_v[i * step : (i + 1) * step, :],
                (((1,), (1,)), ((), ())), preferred_element_type=F32,
            ).astype(BF16)

    project(0)
    pl.semaphore_wait(barrier, len(partners))

    class Unit:
        pass

    units = []
    along_x, along_y = (lambda j: at(dx=j)), (lambda j: at(dy=j))
    for n in range(2 * PARTS):
        u = Unit()
        u.cols = pl.ds((n % 2) * HALF, HALF)
        u.n, u.p, u.w = n, p.at[n // 2, :, u.cols], w.at[n // 2, :, u.cols]
        u.pf = x if n % 2 == 0 else y
        u.first, u.second = (along_x, along_y) if n % 2 == 0 else (along_y, along_x)
        u.r1, u.s1, u.r2 = r1.at[n], s1.at[n], r2.at[n]
        units.append(u)

    def scatter_start(u):
        u.a = [
            send(rows(u.p, ((u.pf + j) % 4) * BLK, BLK), u.r1.at[j - 1],
                 xs.at[u.n, j - 1], xr.at[u.n, j - 1], u.first(j))
            for j in (2, 1, 3)
        ]

    def exchange_start(u):
        total = load(u.p, u.pf * BLK, BLK)
        for copy in u.a:
            copy.wait_recv()
        for j in range(3):
            total = total + u.r1[j].astype(F32)
        u.s1[...] = total.astype(BF16)
        u.b = [
            send(u.s1, u.r2.at[j - 1], xs.at[u.n, 2 + j], xr.at[u.n, 2 + j], u.second(j))
            for j in (2, 1, 3)
        ]

    def gather_start(u):
        for copy in u.b:
            copy.wait_recv()
        mine = pl.ds(pl.multiple_of(u.pf * BLK, 16), BLK)
        for lo in range(0, BLK, ROWS):
            total = u.s1[lo : lo + ROWS, :].astype(F32)
            for j in range(3):
                total = total + u.r2[j, lo : lo + ROWS, :].astype(F32)
            total = total * wrow[:, u.cols]
            u.w[pl.ds(pl.multiple_of(u.pf * BLK + lo, 16), ROWS), :] = total.astype(BF16)
        u.c = [
            send(u.w.at[mine], u.w.at[mine], xs.at[u.n, 5 + j], xr.at[u.n, 5 + j], u.first(j))
            for j in (2, 1, 3)
        ]

    def gather_end(u):
        for copy in u.c:
            copy.wait_recv()

    def units_of(n):
        return units[2 * n : 2 * n + 2]

    for u in units_of(0):
        scatter_start(u)
    project(1)
    for u in units_of(1):
        scatter_start(u)

    f_codes.wait()
    f_ids.wait()
    weights = jnp.where(ids_v[...] == PAD, 0.0, jnp.exp(TEMP * codes_v[...].astype(F32)))
    for i in range(TOK // 128):
        wrow[:, i * 128 : (i + 1) * 128] = jnp.broadcast_to(weights[i : i + 1, :], (ROWS, 128))
    local = jnp.sum(jnp.sum(weights, axis=0, keepdims=True), axis=1, keepdims=True)
    nsend[0] = jnp.broadcast_to(local, (8, 128))
    ncore = send(nsend.at[0], nrecv.at[7], nss.at[7], nrs.at[7], at(dc=1))

    for u in units_of(0):
        exchange_start(u)
    ncore.wait_recv()
    nsend[1] = nsend[0] + nrecv[7]
    sums = [
        send(nsend.at[1], nrecv.at[j - 1], nss.at[j - 1], nrs.at[j - 1], at(dz=j))
        for j in range(1, NZ)
    ]
    for u in units_of(1):
        exchange_start(u)
    for n in range(PARTS):
        for u in units_of(n):
            gather_start(u)
    for copy in sums:
        copy.wait_recv()
    scale = nsend[1]
    for i in range(7):
        scale = scale + nrecv[i]
    scale = TOKENS / scale[0:1, 0:1]
    for copy in f_og + [f_m1, f_m2]:
        copy.wait()

    x0, y0 = dp % NX, dp // NX
    in_row, in_col = y == y0, x == x0
    is_src = jnp.logical_and(in_row, in_col)
    parts = (pl.ds(0, D // 2), pl.ds(D // 2, D // 2))
    hop = ((lambda j: at(dx=j), lambda j: at(dy=j)), (lambda j: at(dy=j), lambda j: at(dx=j)))
    member = (in_row, in_col)

    def spread(h, level, src):
        copies = []
        for j in (1, 2, 3):
            i = h * 6 + level * 3 + j - 1
            copies.append(
                pltpu.make_async_remote_copy(
                    src_ref=src.at[parts[h]], dst_ref=own_v.at[parts[h]],
                    send_sem=bs.at[i], recv_sem=br.at[h],
                    device_id=hop[h][level](j), device_id_type=MESH,
                )
            )
        return copies

    def basis_first():
        @pl.when(is_src)
        def _():
            pltpu.make_async_copy(basis_v, own_v, bl).start()
            for h in (0, 1):
                for copy in spread(h, 0, basis_v):
                    copy.start()
            for h in (0, 1):
                for copy in spread(h, 1, basis_v):
                    copy.start()

    def basis_second():
        for h in (0, 1):
            @pl.when(jnp.logical_and(member[h], jnp.logical_not(is_src)))
            def _(h=h):
                copies = spread(h, 1, own_v)
                copies[0].wait_recv()
                for copy in copies:
                    copy.start()

    def basis_last():
        @pl.when(is_src)
        def _():
            pltpu.make_async_copy(basis_v, own_v, bl).wait()
            for h in (0, 1):
                for copy in spread(h, 0, basis_v):
                    copy.wait_send()

        for h in (0, 1):
            copies = spread(h, 1, own_v)

            @pl.when(jnp.logical_not(member[h]))
            def _(copies=copies):
                copies[0].wait_recv()

            @pl.when(member[h])
            def _(copies=copies):
                for copy in copies:
                    copy.wait_send()

    exch = [[], []]

    def owner(k, core):
        return ((z + k) % NZ) * 2 + core

    def multiply(n):
        for lo in range(0, FF, 128 * 7):
            for at_, width in ((0, 256), (256, 256), (512, 256), (768, 128)):
                part = jnp.dot(
                    w[n], og_v[:, lo + at_ : lo + at_ + width], preferred_element_type=F32
                )
                top = 0 if lo == 0 else 8
                raw[n, :, top : top + 8, at_ : at_ + width] = part.reshape(16, 8, width)
        for i, (at_slot, count) in enumerate(PIECES):
            for k, slot in SLOT.items():
                if at_slot <= slot < at_slot + count:
                    cs[n, slot] = raw[n, owner(k, 1 - c)].astype(BF16)
            span = pl.ds(at_slot, count)
            exch[n].append(
                send(cs.at[n, span], cr.at[n, span], ces.at[n, i], cer.at[n, i], at(dc=1))
            )

    def chip_sum(k, n):
        return raw[n, owner(k, c)] + cr[n, SLOT[k]].astype(F32)

    reduced = [[], []]

    def reduce_send(n, k, to, sem, cols=slice(None)):
        return send(
            tx.at[n, k - 1, :, cols], rx.at[n, k - 1, :, cols], zs.at[n, sem], zr.at[n, sem], at(dz=to)
        )

    relayed = {}

    def reduce_start_relayed(n):
        exch[n][0].wait_recv()
        for k in (4, 3, 5):
            tx[n, k - 1] = chip_sum(k, n).astype(BF16)
            if k == 4:
                relayed[n, "a"] = reduce_send(n, 4, 2, 3, LEFT)
                relayed[n, "b"] = reduce_send(n, 4, 6, 7, RIGHT)
            else:
                relayed[n, k] = reduce_send(n, k, 1 if k == 3 else 7, k - 1)
        exch[n][1].wait_recv()
        exch[n][2].wait_recv()
        for k in (1, 7):
            tx[n, k - 1] = chip_sum(k, n).astype(BF16)
            reduced[n].append(reduce_send(n, k, k, k - 1))

    def reduce_relay(n):
        for k, near, far, cols in ((2, 3, "a", LEFT), (6, 5, "b", RIGHT)):
            relayed[n, near].wait_recv()
            relayed[n, far].wait_recv()
            total = chip_sum(k, n) + rx[n, near - 1].astype(F32)
            tx[n, k - 1] = total.astype(BF16)
            more = total[:, cols.start : cols.start + cols.size] + rx[n, 3, :, cols].astype(F32)
            tx[n, k - 1, :, cols] = more.astype(BF16)
            reduced[n].append(reduce_send(n, k, k, k - 1))

    def reduce_start(n):
        for i, offsets in enumerate(((4, 3, 5), (2, 6), (1, 7))):
            exch[n][i].wait_recv()
            for k in offsets:
                tx[n, k - 1] = chip_sum(k, n).astype(BF16)
                reduced[n].append(
                    send(tx.at[n, k - 1], rx.at[n, k - 1], zs.at[n, k - 1], zr.at[n, k - 1], at(dz=k))
                )

    bias1 = 1.0 - B1**ADAM_STEP
    bias2 = 1.0 - B2**ADAM_STEP
    forwards, gathered = {}, {}

    def forward(n, off):
        block = up.at[n, ((z + off) % NZ) * 2 + c]
        forwards[n, off] = send(block, block, fs.at[n, off], fr.at[n, off], at(dc=1))

    def gather_relay(n):
        for k, near, half, cols in ((2, 3, 4, LEFT), (6, 5, 0, RIGHT)):
            gathered[n, k].wait_recv()
            block = up.at[n, ((z + NZ - k) % NZ) * 2 + c]
            part = up.at[n, ((z + NZ - k) % NZ) * 2 + c, :, cols]
            gathered[n, half] = send(part, part, gs.at[n, half], gr.at[n, half], at(dz=k))
            gathered[n, near] = send(
                block, block, gs.at[n, near], gr.at[n, near], at(dz=1 if k == 2 else NZ - 1)
            )

    def adam(n):
        for copy in reduced[n]:
            copy.wait_recv()
        grad = chip_sum(0, n)
        for k in (0, 1, 5, 6) if n in SUM_RELAY else range(NZ - 1):
            grad = grad + rx[n, k].astype(F32)
        grad = grad * scale
        first = B1 * side_by_side(m1_v, n) + (1.0 - B1) * grad
        second = B2 * side_by_side(m2_v, n) + (1.0 - B2) * grad * grad
        up[n, dp] = ((first / bias1) / (jnp.sqrt(second / bias2) + EPS)).astype(BF16)
        block = up.at[n, dp]
        for k in (2, 6, 1, 7) if n in GATHER_RELAY else (4, 3, 5, 2, 6, 1, 7):
            gathered[n, k] = send(block, block, gs.at[n, k], gr.at[n, k], at(dz=k))
        forward(n, 0)
        for ref, value in ((nf_v, first), (ns_v, second)):
            ref[n * 8 : n * 8 + 8, 0:SIDE] = value[0:8]
            ref[n * 8 : n * 8 + 8, SIDE:FF] = value[8:16]

    for n in range(PARTS):
        for u in units_of(n):
            gather_end(u)
        multiply(n)
        early = len(pending)
        if n in SUM_RELAY:
            reduce_start_relayed(n)
        else:
            reduce_start(n)
    basis_first()
    drain(early)
    early = len(pending)
    for n in range(PARTS):
        if n in SUM_RELAY:
            reduce_relay(n)
    for n in range(PARTS):
        adam(n)
    basis_second()
    drain(early)
    for n in range(PARTS):
        if n in GATHER_RELAY:
            gather_relay(n)
    for n in range(PARTS):
        if n in GATHER_RELAY:
            for k in (1, 7):
                gathered[n, k].wait_recv()
                forward(n, NZ - k)
            for k in (2, 6):
                forward(n, NZ - k)
            for k in (3, 5):
                gathered[n, k].wait_recv()
                forward(n, NZ - k)
            gathered[n, 4].wait_recv()
            gathered[n, 0].wait_recv()
            forward(n, 4)
        else:
            for k in (1, 7, 2, 6, 3, 5, 4):
                gathered[n, k].wait_recv()
                forward(n, NZ - k)
    basis_last()
    for n in range(PARTS):
        for off in range(NZ):
            forwards[n, off].wait_recv()
    for copy in pending:
        copy.wait_send()


def final_kernel(nf_v, ns_v, own_v, up, nf_o, ns_o, wu_o, wu_v, osem):
    copies = [
        pltpu.make_async_copy(nf_v, nf_o, osem.at[0]),
        pltpu.make_async_copy(ns_v, ns_o, osem.at[1]),
    ]
    for copy in copies:
        copy.start()
    n = 2
    for h in (0, 1):
        for at_, width in ((0, 256), (256, 256), (512, 256), (768, 128)):
            lines = [
                up[i, :, :, at_ : at_ + width].astype(F32)[:, h * 8 : h * 8 + 8] for i in range(PARTS)
            ]
            lines = jnp.concatenate(lines, axis=1).astype(BF16).reshape(R, width)
            lo = h * SIDE + at_
            cols = pl.ds(lo, width)
            wu_v[:, lo : lo + width] = jnp.dot(
                own_v[...], lines, preferred_element_type=F32
            ).astype(BF16)
            copies.append(pltpu.make_async_copy(wu_v.at[:, cols], wu_o.at[:, cols], osem.at[n]))
            copies[-1].start()
            n += 1
    for copy in copies:
        copy.wait()


def local(activations, out_grads, basis, first_moment, second_moment, reward_codes, token_ids):
    hbm = pl.BlockSpec(memory_space=pltpu.HBM)
    near = pl.BlockSpec(memory_space=pltpu.VMEM)
    vm = pltpu.VMEM
    dma = pltpu.SemaphoreType.DMA
    moments = jax.ShapeDtypeStruct((ROWS, FF), F32)
    states = pl.pallas_call(
        kernel,
        out_shape=(
            vm((ROWS, FF), F32),
            vm((ROWS, FF), F32),
            vm((D, R), BF16),
            vm((PARTS, 16, ROWS, SIDE), BF16),
        ),
        in_specs=[hbm] * 7,
        out_specs=(near,) * 4,
        scratch_shapes=[
            vm((TOK, D), BF16), vm((TOK, FF), BF16), vm((D, R), BF16), vm((R, D), BF16),
            vm((ROWS, FF), F32), vm((ROWS, FF), F32),
            vm((TOK // 128, 128), jnp.int32), vm((TOK // 128, 128), jnp.int32),
            vm((ROWS, TOK), F32),
            vm((PARTS, RP, TOK), BF16), vm((PARTS, RP, TOK), BF16),
            vm((2 * PARTS, 3, BLK, HALF), BF16), vm((2 * PARTS, BLK, HALF), BF16),
            vm((2 * PARTS, 3, BLK, HALF), BF16), vm((PARTS, 16, ROWS, SIDE), F32),
            vm((2, 8, 128), F32), vm((8, 8, 128), F32),
            vm((PARTS, 8, ROWS, SIDE), BF16), vm((PARTS, 8, ROWS, SIDE), BF16),
            vm((PARTS, 8, ROWS, SIDE), BF16), vm((PARTS, 8, ROWS, SIDE), BF16),
            dma((13,)), dma((2 * PARTS, 9)), dma((2 * PARTS, 9)), dma((8,)), dma((8,)),
            dma((2, 3)), dma((2, 3)), dma((2, 8)), dma((2, 8)), dma((2, 8)), dma((2, 8)),
            dma((2, 8)), dma((2, 8)), dma((12,)), dma((2,)), dma,
        ],
        compiler_params=pltpu.CompilerParams(
            collective_id=0, has_side_effects=True, vmem_limit_bytes=55_260_000
        ),
        name="galore_step",
    )(
        activations, out_grads, basis, first_moment, second_moment,
        reward_codes.reshape(TOK // 128, 128), token_ids.reshape(TOK // 128, 128),
    )
    return pl.pallas_call(
        final_kernel,
        out_shape=(moments, moments, jax.ShapeDtypeStruct((D, FF), BF16)),
        in_specs=[near] * 4,
        out_specs=(hbm, hbm, hbm),
        scratch_shapes=[vm((D, FF), BF16), dma((10,))],
        compiler_params=pltpu.CompilerParams(vmem_limit_bytes=16 * 1024 * 1024),
        name="project_back",
    )(*states)


def solution(mesh):
    return jax.shard_map(
        local,
        mesh=mesh,
        in_specs=(
            P("dp", "tensor"),
            P("dp", "tensor"),
            P("tensor", None),
            P("dp", "tensor"),
            P("dp", "tensor"),
            P("dp"),
            P("dp"),
        ),
        out_specs=(P("dp", "tensor"), P("dp", "tensor"), P("dp", "tensor")),
        check_vma=False,
    )
```
